32 devices in a mesh: seq: 8 (over z, x), tp: 4 (over y, core).
Axes of the slice: x: 2, y: 2, z: 4, core: 2. Of those that a mesh axis runs over, the one named last changes fastest.
Arguments:
- queries: bfloat16 [2048, 4096], P('seq', 'tp'), may hold values from -6 to 6
- keys: bfloat16 [2048, 4096], P('seq', 'tp'), may hold values from -6 to 6
- values: bfloat16 [2048, 4096], P('seq', 'tp'), may hold values from -12 to 12
- seeds: bfloat16 [32, 256], P('tp'), may hold values from -6 to 6
- gain: float32 [4096], P('tp'), may hold values from 0.1 to 1.9
Outputs:
- attended: bfloat16 [2048, 4096], P('seq', 'tp')
The draws below stay inside these ranges and needn't reach their ends.
All inputs are finite; a program needn't handle non-finite values.
Results may differ from the reference program's by a relative error of at most 0.009.
Values sent between devices are 32-bit elements; how exact they have to be, the bound alone decides.
No kernel may reach another device: no remote copies, remote signals or barrier semaphores. Data moves between devices by JAX's collectives and lax.ppermute only.
A program may use at most 192 MiB of HBM per device.

```python
import jax
import jax.numpy as jnp
from jax import lax

H = 32
E = 128
M = 256
TOKENS = 2048


def draw_values(key, part):
    head = (jnp.arange(H * E) // E).astype(jnp.float32)
    scale = 1.0 + 2.0 * head / (H - 1)
    base = jax.random.truncated_normal(key, -4.0, 4.0, (TOKENS, H * E), jnp.float32)
    return (base * scale[None, :]).astype(jnp.bfloat16)


def block_levels(key, dims, split, smallest, largest):
    factor_of, own = 1.0, jax.random.fold_in(key, 6)
    for dim, parts in split:
        heights = jnp.exp(jax.random.uniform(jax.random.fold_in(own, dim), (parts,), jnp.float32, smallest / len(split), largest / len(split)))
        factor_of = factor_of * jnp.repeat(heights, dims[dim] // parts).reshape([-1 if axis == dim else 1 for axis in range(len(dims))])
    return factor_of


def scatter_about(stream_key, dims, scale, most, pieces=(), kind=jnp.bfloat16):
    entries = scale * jax.random.normal(stream_key, dims, jnp.float32)
    if pieces:
        entries = entries * block_levels(stream_key, dims, pieces, -0.22, 0.18)
    return jnp.clip(entries, -most, most).astype(kind)


def setup_inputs(seed: int = 0) -> dict:
    splits = jax.random.split(jax.random.key(seed), 6)
    queries = scatter_about(splits[0], (TOKENS, H * E), 1.0, 6.0, ((0, 8), (1, 4)))
    keys = scatter_about(splits[1], (TOKENS, H * E), 1.0, 6.0, ((0, 8), (1, 4)))
    values = draw_values(jax.random.fold_in(splits[5], 71), 0)
    seeds = scatter_about(splits[3], (H, M), 1.0, 6.0, ((0, 4),))
    gain = jnp.clip(1.0 + 0.18 * jax.random.normal(splits[4], (H * E,), jnp.float32), 0.1, 1.9)
    return {"queries": queries, "keys": keys, "values": values, "seeds": seeds, "gain": gain}


def features(rows, seeds):
    count = rows.shape[0]
    x = rows.astype(jnp.float32).reshape(count, H, E)
    blocks = seeds.astype(jnp.float32).reshape(H, M // E, E)
    spectrum = jnp.fft.fft(blocks)[None] * jnp.fft.fft(x)[:, :, None, :]
    mixed = jnp.real(jnp.fft.ifft(spectrum)).reshape(count, H, M) * E ** (-0.25)
    return (jax.nn.elu(mixed) + 1.0).astype(jnp.bfloat16)

def reference(queries, keys, values, seeds, gain):
    block = min(512, TOKENS)
    steps_count = TOKENS // block
    q_blocks = queries.reshape(steps_count, block, H * E)
    k_blocks = keys.reshape(steps_count, block, H * E)
    v_blocks = values.reshape(steps_count, block, H * E)
    causal = jnp.tril(jnp.ones((block, block), dtype=bool))
    high = lax.Precision.HIGHEST

    def advance(carry, inputs):
        state, totals = carry
        q_rows, k_rows, v_rows = inputs
        fq = features(q_rows, seeds).astype(jnp.float32)
        fk = features(k_rows, seeds).astype(jnp.float32)
        vals = v_rows.astype(jnp.float32).reshape(block, H, E)
        scores = jnp.einsum('bhm,chm->hbc', fq, fk, precision=high)
        scores = jnp.where(causal[None], scores, 0.0)
        wscores = lax.optimization_barrier(scores.astype(jnp.bfloat16)).astype(jnp.float32)
        num = jnp.einsum('hbc,che->bhe', wscores, vals, precision=high)
        num = num + jnp.einsum('bhm,hme->bhe', fq, state, precision=high)
        den = lax.optimization_barrier(jnp.sum(scores, axis=2)).T + jnp.einsum('bhm,hm->bh', fq, totals, precision=high)
        heads = num / den[:, :, None]
        meansq = lax.optimization_barrier(jnp.mean(heads * heads, axis=(1, 2)))
        normed = heads.reshape(block, H * E) * lax.rsqrt(meansq + 1e-06)[:, None] * gain[None, :]
        state = state + jnp.einsum('chm,che->hme', fk, vals, precision=high)
        totals = totals + lax.optimization_barrier(jnp.sum(fk, axis=0))
        return ((state, totals), normed.astype(jnp.bfloat16))
    start = (jnp.zeros((H, M, E), jnp.float32), jnp.zeros((H, M), jnp.float32))
    _, outputs = lax.scan(advance, start, (q_blocks, k_blocks, v_blocks))
    return outputs.reshape(TOKENS, H * E)
```

```python
import functools

import jax
import jax.numpy as jnp
from jax import lax
from jax.experimental import pallas as pl
from jax.experimental.pallas import tpu as pltpu
from jax.sharding import PartitionSpec as P

WIDTH = 128
NT = (((1,), (1,)), ((), ()))
TN = (((0,), (0,)), ((), ()))
VMEM = pl.BlockSpec(memory_space=pltpu.VMEM)
SMEM = pl.BlockSpec(memory_space=pltpu.SMEM)
PARAMS = pltpu.CompilerParams(vmem_limit_bytes=24 * 2**20)


def rotated(seeds_ref, first):
    heads = seeds_ref.shape[0]
    seeds = seeds_ref[...].astype(jnp.float32)
    return pltpu.roll(seeds, lax.rem(heads - first, heads), 0)


def table_of(seeds, i, group):
    row = seeds[i : i + 1, group * WIDTH : (group + 1) * WIDTH]
    square = jnp.broadcast_to(row, (WIDTH, WIDTH))
    return pltpu.roll(square, 0, 1, stride=1, stride_axis=0).astype(jnp.bfloat16)


def phi(x, table):
    mixed = jnp.dot(x, table, preferred_element_type=jnp.float32) * WIDTH ** (-0.25)
    return (jnp.exp(jnp.minimum(mixed, 0.0)) + jnp.maximum(mixed, 0.0)).astype(jnp.bfloat16)


def features(x, seeds, i):
    groups = seeds.shape[1] // WIDTH
    return jnp.concatenate([phi(x, table_of(seeds, i, g)) for g in range(groups)], axis=1)


def columns(head):
    return pl.ds(pl.multiple_of(head * WIDTH, WIDTH), WIDTH)


def state_kernel(half, first_ref, seeds_ref, k_ref, v_ref, *outs):
    first = first_ref[0]
    seeds = rotated(seeds_ref, first)
    for i in range(half):
        head = first + i
        fk = features(k_ref[:, columns(head)], seeds, i)
        vals = v_ref[:, columns(head)]
        outs[i][0:WIDTH, :] = lax.dot_general(vals, fk, TN, preferred_element_type=jnp.float32)
        outs[0][WIDTH + i : WIDTH + i + 1, :] = jnp.sum(
            fk.astype(jnp.float32), axis=0, keepdims=True
        )


def local_kernel(first_ref, seeds_ref, q_ref, k_ref, v_ref, num_ref, den_ref, fq_ref):
    seeds = rotated(seeds_ref, first_ref[0])
    heads = seeds_ref.shape[0]
    feats = seeds_ref.shape[1]
    tok = q_ref.shape[0]
    rows = lax.broadcasted_iota(jnp.int32, (tok, tok), 0)
    causal = lax.broadcasted_iota(jnp.int32, (tok, tok), 1) <= rows
    for i in range(heads):
        head = lax.rem(first_ref[0] + i, heads)
        fk = features(k_ref[:, columns(head)], seeds, i)
        fq = features(q_ref[:, columns(head)], seeds, i)
        fq_ref[:, i * feats : (i + 1) * feats] = fq
        scores = lax.dot_general(fq, fk, NT, preferred_element_type=jnp.float32)
        scores = jnp.where(causal, scores, 0.0)
        num_ref[:, i * WIDTH : (i + 1) * WIDTH] = jnp.dot(
            scores.astype(jnp.bfloat16),
            v_ref[:, columns(head)],
            preferred_element_type=jnp.float32,
        )
        den_ref[:, i * WIDTH : (i + 1) * WIDTH] = jnp.broadcast_to(
            jnp.sum(scores, axis=1, keepdims=True), (tok, WIDTH)
        )


def join_kernel(half, offset, fq_ref, num_ref, den_ref, *refs):
    states, (heads_ref, squares_ref) = refs[:half], refs[half:]
    feats = states[0].shape[1]
    tok = fq_ref.shape[0]
    squares = jnp.zeros((tok, WIDTH), jnp.float32)
    for i in range(half):
        at = offset + i
        total = states[0][WIDTH + i : WIDTH + i + 1, :]
        wide = jnp.concatenate(
            [states[i][0:WIDTH, :], jnp.broadcast_to(total, (WIDTH, feats))], axis=0
        )
        upper = wide.astype(jnp.bfloat16)
        lower = (wide - upper.astype(jnp.float32)).astype(jnp.bfloat16)
        fq = fq_ref[:, at * feats : (at + 1) * feats]
        both = lax.dot_general(fq, upper, NT, preferred_element_type=jnp.float32)
        both = both + lax.dot_general(fq, lower, NT, preferred_element_type=jnp.float32)
        num = num_ref[:, at * WIDTH : (at + 1) * WIDTH] + both[:, :WIDTH]
        den = den_ref[:, at * WIDTH : (at + 1) * WIDTH] + both[:, WIDTH:]
        head = num / den
        heads_ref[:, i * WIDTH : (i + 1) * WIDTH] = head
        squares = squares + head * head
    rows = jnp.broadcast_to(jnp.sum(squares, axis=1, keepdims=True), (tok, WIDTH))
    squares_ref[...] = rows.T[0:8, :]


def norm_kernel(half, entries, first_ref, gain_ref, own_ref, other_ref, *refs):
    squares, out_ref = refs[:-1], refs[-1]
    tok = own_ref.shape[0]
    overall = functools.reduce(lambda a, b: a + b, [ref[...] for ref in squares])
    factor = lax.rsqrt(overall / entries + 1e-06)
    wide = jnp.broadcast_to(factor[0:1, :], (WIDTH, tok)).T
    for part, source in enumerate((own_ref, other_ref)):
        for i in range(half):
            head = lax.rem(first_ref[0] + part * half + i, 2 * half)
            at = columns(head)
            out_ref[:, at] = (
                source[:, i * WIDTH : (i + 1) * WIDTH] * wide * gain_ref[:, at]
            ).astype(jnp.bfloat16)


def call(kernel, outs, ins, scalars, flops):
    moved = sum(x.size * x.dtype.itemsize for x in ins)
    moved += sum(x.size * jnp.dtype(x.dtype).itemsize for x in jax.tree.leaves(outs))
    return pl.pallas_call(
        kernel,
        out_shape=outs,
        in_specs=[SMEM] * scalars + [VMEM] * (len(ins) - scalars),
        out_specs=jax.tree.map(lambda _: VMEM, outs),
        compiler_params=PARAMS,
        cost_estimate=pl.CostEstimate(flops=flops, bytes_accessed=moved, transcendentals=0),
    )(*ins)


def per_device(queries, keys, values, seeds, gain):
    f32 = jnp.float32
    tok = queries.shape[0]
    heads, feats = seeds.shape
    half = heads // 2
    count = lax.axis_size("seq")
    pairs = count // 2
    mine = lax.axis_index("seq")
    side = lax.rem(mine, 2)
    own_first = (side * half).reshape(1)
    other_first = ((1 - side) * half).reshape(1)
    shape = lambda *dims, dtype=f32: jax.ShapeDtypeStruct(dims, dtype)

    state_shapes = [shape(WIDTH + (8 if i == 0 else 0), feats) for i in range(half)]
    states = lambda first: call(
        functools.partial(state_kernel, half),
        state_shapes,
        (first, seeds, keys, values),
        1,
        half * tok * feats * WIDTH * 4,
    )
    theirs = states(other_first)
    ours = states(own_first)

    swap = [(i, i ^ 1) for i in range(count)]
    hops = [[(2 * p, 2 * p + 2), (2 * p + 1, 2 * p + 3)] for p in range(pairs - 1)]
    incoming = [lax.ppermute(part, "seq", swap) for part in theirs]
    totals = [a + b for a, b in zip(ours, incoming)]
    num, den, fq = call(
        local_kernel,
        [shape(tok, heads * WIDTH), shape(tok, heads * WIDTH), shape(tok, heads * feats, dtype=jnp.bfloat16)],
        (own_first, seeds, queries, keys, values),
        1,
        heads * tok * (feats * WIDTH * 4 + tok * (feats + WIDTH) * 2),
    )
    own_prior, passed = [], []
    for i in range(half):
        prior = jnp.zeros_like(totals[i])
        arrived = prior
        for hop in hops:
            arrived = lax.ppermute(arrived + totals[i], "seq", hop)
            prior = prior + arrived
        passed.append(lax.ppermute(prior + jnp.where(side == 0, ours[i], 0.0), "seq", swap))
        own_prior.append(prior + jnp.where(side == 0, 0.0, incoming[i]))
    join = lambda offset, prior: call(
        functools.partial(join_kernel, half, offset),
        [shape(tok, half * WIDTH), shape(8, tok)],
        (fq, num, den, *prior),
        0,
        half * tok * feats * WIDTH * 8,
    )
    own_heads, own_squares = join(0, own_prior)
    other_heads, other_squares = join(half, passed)
    squares = own_squares + other_squares
    across = lax.axis_size("tp")
    gathered = [squares] + [
        lax.ppermute(squares, "tp", [(i, (i + k) % across) for i in range(across)])
        for k in range(1, across)
    ]
    return call(
        functools.partial(norm_kernel, half, heads * WIDTH * across),
        shape(tok, heads * WIDTH, dtype=jnp.bfloat16),
        (own_first, gain.reshape(1, -1), own_heads, other_heads, *gathered),
        1,
        tok * heads * WIDTH * 3,
    )


def solution(mesh):
    placed = (P("seq", "tp"), P("seq", "tp"), P("seq", "tp"), P("tp", None), P("tp"))
    return jax.shard_map(
        per_device, mesh=mesh, in_specs=placed, out_specs=P("seq", "tp"), check_vma=False
    )
```

```python
import functools

import jax
import jax.numpy as jnp
from jax import lax
from jax.experimental import pallas as pl
from jax.experimental.pallas import tpu as pltpu
from jax.sharding import PartitionSpec as P

WIDTH = 128
NT = (((1,), (1,)), ((), ()))
TN = (((0,), (0,)), ((), ()))
VMEM = pl.BlockSpec(memory_space=pltpu.VMEM)
HBM = pl.BlockSpec(memory_space=pltpu.HBM)
ANY = pl.BlockSpec(memory_space=pl.ANY)
SMEM = pl.BlockSpec(memory_space=pltpu.SMEM)
MIB = 2**20


def rotated(seeds_ref, first):
    heads = seeds_ref.shape[0]
    seeds = seeds_ref[...].astype(jnp.float32)
    return pltpu.roll(seeds, lax.rem(heads - first, heads), 0)


def table_of(seeds, i, group):
    row = seeds[i : i + 1, group * WIDTH : (group + 1) * WIDTH]
    square = jnp.broadcast_to(row, (WIDTH, WIDTH))
    return pltpu.roll(square, 0, 1, stride=1, stride_axis=0).astype(jnp.bfloat16)


def phi(x, table):
    mixed = jnp.dot(x, table, preferred_element_type=jnp.float32) * WIDTH ** (-0.25)
    return (jnp.exp(jnp.minimum(mixed, 0.0)) + jnp.maximum(mixed, 0.0)).astype(jnp.bfloat16)


def features(x, seeds, i):
    groups = seeds.shape[1] // WIDTH
    return jnp.concatenate([phi(x, table_of(seeds, i, g)) for g in range(groups)], axis=1)


def columns(head):
    return pl.ds(pl.multiple_of(head * WIDTH, WIDTH), WIDTH)


def state_kernel(half, first_ref, seeds_hbm, k_hbm, v_hbm, *refs):
    outs, (seeds_ref, k_ref, v_ref, sems) = refs[:half], refs[half:]
    first = first_ref[0]
    span = pl.ds(pl.multiple_of(first * WIDTH, WIDTH), half * WIDTH)
    copies = [
        pltpu.make_async_copy(seeds_hbm, seeds_ref, sems.at[0]),
        pltpu.make_async_copy(k_hbm.at[:, span], k_ref, sems.at[1]),
        pltpu.make_async_copy(v_hbm.at[:, span], v_ref, sems.at[2]),
    ]
    for copy in copies:
        copy.start()
    copies[0].wait()
    seeds = rotated(seeds_ref, first)
    outs[0][WIDTH:, :] = jnp.zeros((outs[0].shape[0] - WIDTH, outs[0].shape[1]), jnp.float32)
    copies[1].wait()
    copies[2].wait()
    for i in range(half):
        at = slice(i * WIDTH, (i + 1) * WIDTH)
        fk = features(k_ref[:, at], seeds, i)
        outs[i][0:WIDTH, :] = lax.dot_general(
            v_ref[:, at], fk, TN, preferred_element_type=jnp.float32
        )
        outs[0][WIDTH + i : WIDTH + i + 1, :] = jnp.sum(
            fk.astype(jnp.float32), axis=0, keepdims=True
        )


def local_kernel(places, first_ref, seeds_ref, q_ref, k_ref, v_ref, *outs):
    seeds = rotated(seeds_ref, first_ref[0])
    heads = seeds_ref.shape[0]
    tok = q_ref.shape[0]
    rows = lax.broadcasted_iota(jnp.int32, (tok, tok), 0)
    causal = lax.broadcasted_iota(jnp.int32, (tok, tok), 1) <= rows
    for n, i in enumerate(places):
        num_ref, den_ref, fq_ref = outs[3 * n : 3 * n + 3]
        head = lax.rem(first_ref[0] + i, heads)
        fk = features(k_ref[:, columns(head)], seeds, i)
        fq = features(q_ref[:, columns(head)], seeds, i)
        fq_ref[...] = fq
        scores = lax.dot_general(fq, fk, NT, preferred_element_type=jnp.float32)
        scores = jnp.where(causal, scores, 0.0)
        num_ref[...] = jnp.dot(
            scores.astype(jnp.bfloat16),
            v_ref[:, columns(head)],
            preferred_element_type=jnp.float32,
        )
        den_ref[...] = jnp.broadcast_to(jnp.sum(scores, axis=1, keepdims=True), (tok, WIDTH))


def join_kernel(i, *refs):
    ins, (own_ref, other_ref, squares_ref) = refs[:-3], refs[-3:]
    squares = jnp.zeros(own_ref.shape, jnp.float32)
    for n, out_ref in enumerate((own_ref, other_ref)):
        num_ref, den_ref, fq_ref, state_ref, totals_ref = ins[5 * n : 5 * n + 5]
        total = totals_ref[WIDTH + i : WIDTH + i + 1, :]
        wide = jnp.concatenate(
            [state_ref[0:WIDTH, :], jnp.broadcast_to(total, (WIDTH, total.shape[1]))], axis=0
        )
        upper = wide.astype(jnp.bfloat16)
        lower = (wide - upper.astype(jnp.float32)).astype(jnp.bfloat16)
        fq = fq_ref[...]
        both = lax.dot_general(fq, upper, NT, preferred_element_type=jnp.float32)
        both = both + lax.dot_general(fq, lower, NT, preferred_element_type=jnp.float32)
        head = (num_ref[...] + both[:, :WIDTH]) / (den_ref[...] + both[:, WIDTH:])
        out_ref[...] = head
        squares = squares + head * head
    rows = jnp.broadcast_to(jnp.sum(squares, axis=1, keepdims=True), squares.shape)
    squares_ref[...] = rows.T[0:8, :]
    if len(ins) > 10:
        squares_ref[...] += ins[10][...]


def norm_kernel(half, entries, first_ref, gain_ref, *refs):
    heads, squares, out_ref = refs[: 2 * half], refs[2 * half : -1], refs[-1]
    tok = out_ref.shape[0]
    overall = functools.reduce(lambda a, b: a + b, [ref[...] for ref in squares])
    factor = lax.rsqrt(overall / entries + 1e-06)
    wide = jnp.broadcast_to(factor[0:1, :], (WIDTH, tok)).T
    for i, source in enumerate(heads):
        at = columns(lax.rem(first_ref[0] + i, 2 * half))
        out_ref[:, at] = (source[...] * wide * gain_ref[:, at]).astype(jnp.bfloat16)


def first_kernel(flag_ref, _, ours_ref, incoming_ref, totals_ref, extra_ref):
    totals_ref[...] = ours_ref[...] + incoming_ref[...]
    extra_ref[...] = jnp.where(flag_ref[0] == 0, ours_ref[...], incoming_ref[...])


def hop_kernel(flag_ref, _, arrived_ref, totals_ref, *refs):
    sent_ref, prior_ref = refs[-2:]
    sent_ref[...] = arrived_ref[...] + totals_ref[...]
    prior_ref[...] = arrived_ref[...] + (refs[0][...] if len(refs) > 2 else 0.0)


def last_kernel(flag_ref, _, arrived_ref, extra_ref, *refs):
    passed_ref, own_ref = refs[-2:]
    prior = arrived_ref[...] + (refs[0][...] if len(refs) > 2 else 0.0)
    more = prior + extra_ref[...]
    passed_ref[...] = jnp.where(flag_ref[0] == 0, more, prior)
    own_ref[...] = jnp.where(flag_ref[0] == 0, prior, more)


def call(kernel, outs, ins, scalars, flops, scratch=(), place=VMEM, limit=16 * MIB, unused=0):
    moved = sum(x.size * x.dtype.itemsize for x in ins)
    moved += sum(x.size * jnp.dtype(x.dtype).itemsize for x in jax.tree.leaves(outs))
    return pl.pallas_call(
        kernel,
        out_shape=outs,
        in_specs=[SMEM] * scalars + [ANY] * unused + [place] * (len(ins) - scalars - unused),
        out_specs=jax.tree.map(lambda _: VMEM, outs),
        scratch_shapes=list(scratch),
        compiler_params=pltpu.CompilerParams(vmem_limit_bytes=limit),
        cost_estimate=pl.CostEstimate(flops=flops, bytes_accessed=moved, transcendentals=0),
    )(*ins)


def per_device(queries, keys, values, seeds, gain):
    f32 = jnp.float32
    tok = queries.shape[0]
    heads, feats = seeds.shape
    half = heads // 2
    count = lax.axis_size("seq")
    pairs = count // 2
    mine = lax.axis_index("seq")
    side = lax.rem(mine, 2)
    own_first = (side * half).reshape(1)
    other_first = ((1 - side) * half).reshape(1)
    shape = lambda *dims, dtype=f32: jax.ShapeDtypeStruct(dims, dtype)

    state_shapes = [shape(WIDTH + (8 if i == 0 else 0), feats) for i in range(half)]
    part = pltpu.VMEM((tok, half * WIDTH), keys.dtype)
    states = lambda first, limit: call(
        functools.partial(state_kernel, half),
        state_shapes,
        (first, seeds, keys, values),
        1,
        half * tok * feats * WIDTH * 4,
        [pltpu.VMEM((heads, feats), seeds.dtype), part, part, pltpu.SemaphoreType.DMA((3,))],
        HBM,
        limit,
    )
    theirs = states(other_first, 60 * MIB)
    ours = states(own_first, 40 * MIB)

    swap = [(i, i ^ 1) for i in range(count)]
    hops = [[(2 * p, 2 * p + 2), (2 * p + 1, 2 * p + 3)] for p in range(pairs - 1)]
    incoming = [lax.ppermute(part, "seq", swap) for part in theirs]
    totals, extra, prior = [None] * half, [None] * half, [None] * half
    arrived, own_prior, passed = [None] * half, [None] * half, [None] * half
    flag = side.reshape(1)
    last = flag
    for slot in range(half + len(hops)):
        for stage in range(len(hops) + 1):
            i = slot - stage
            if not 0 <= i < half:
                continue
            like = jax.ShapeDtypeStruct(ours[i].shape, f32)
            glue = lambda kernel, *ins: call(kernel, [like, like], (flag, last, *ins), 1, 10**9, unused=1)
            if stage == 0:
                totals[i], extra[i] = glue(first_kernel, ours[i], incoming[i])
                sent = totals[i]
            elif stage < len(hops):
                sent, prior[i] = glue(hop_kernel, arrived[i], totals[i], *([prior[i]] if stage > 1 else []))
            else:
                sent, own_prior[i] = glue(last_kernel, arrived[i], extra[i], *([prior[i]] if stage > 1 else []))
            last = sent
            if stage < len(hops):
                arrived[i] = lax.ppermute(sent, "seq", hops[stage])
            else:
                passed[i] = lax.ppermute(sent, "seq", swap)
    bf16 = jnp.bfloat16
    local_shapes = [shape(tok, WIDTH), shape(tok, WIDTH), shape(tok, feats, dtype=bf16)]
    own_heads, other_heads, squares = [], [], None
    for i in range(half):
        parts = call(
            functools.partial(local_kernel, (i, half + i)),
            local_shapes * 2,
            (own_first, seeds, queries, keys, values),
            1,
            2 * tok * (feats * WIDTH * 4 + tok * (feats + WIDTH) * 2),
        )
        joined = (*parts[:3], own_prior[i], own_prior[0], *parts[3:], passed[i], passed[0])
        own, other, squares = call(
            functools.partial(join_kernel, i),
            [shape(tok, WIDTH), shape(tok, WIDTH), shape(8, tok)],
            joined if squares is None else (*joined, squares),
            0,
            2 * tok * feats * WIDTH * 8,
        )
        own_heads.append(own)
        other_heads.append(other)
    across = lax.axis_size("tp")
    gathered = [squares] + [
        lax.ppermute(squares, "tp", [(i, (i + k) % across) for i in range(across)])
        for k in range(1, across)
    ]
    return call(
        functools.partial(norm_kernel, half, heads * WIDTH * across),
        shape(tok, heads * WIDTH, dtype=jnp.bfloat16),
        (own_first, gain.reshape(1, -1), *own_heads, *other_heads, *gathered),
        1,
        tok * heads * WIDTH * 3,
    )


def solution(mesh):
    placed = (P("seq", "tp"), P("seq", "tp"), P("seq", "tp"), P("tp", None), P("tp"))
    return jax.shard_map(
        per_device, mesh=mesh, in_specs=placed, out_specs=P("seq", "tp"), check_vma=False
    )
```

```python
import functools

import jax
import jax.numpy as jnp
from jax import lax
from jax.experimental import pallas as pl
from jax.experimental.pallas import tpu as pltpu
from jax.sharding import PartitionSpec as P

WIDTH = 128
MIB = 2**20
DIRECTS = (1, 1)
CROSSES = ()
PARTS = 3
GLUE_COST = 10**9
GAP = 2.1
ORDER = None


NT = (((1,), (1,)), ((), ()))
TN = (((0,), (0,)), ((), ()))
VMEM = pl.BlockSpec(memory_space=pltpu.VMEM)
HBM = pl.BlockSpec(memory_space=pltpu.HBM)
ANY = pl.BlockSpec(memory_space=pl.ANY)
SMEM = pl.BlockSpec(memory_space=pltpu.SMEM)


def first_of(group, half, mine_ref):
    side = lax.rem(mine_ref[0], 2)
    return half * (side if group == 0 else 1 - side)


def rotated(seeds, first):
    heads = seeds.shape[0]
    return pltpu.roll(seeds, lax.rem(heads - first, heads), 0)


def table_of(row):
    square = jnp.broadcast_to(row, (WIDTH, WIDTH))
    return pltpu.roll(square, 0, 1, stride=1, stride_axis=0).astype(jnp.bfloat16)


def phi(x, table):
    mixed = jnp.dot(x, table, preferred_element_type=jnp.float32) * WIDTH ** (-0.25)
    return (jnp.exp(jnp.minimum(mixed, 0.0)) + jnp.maximum(mixed, 0.0)).astype(jnp.bfloat16)


def features(x, seeds, i):
    groups = seeds.shape[1] // WIDTH
    rows = [seeds[i : i + 1, g * WIDTH : (g + 1) * WIDTH] for g in range(groups)]
    return jnp.concatenate([phi(x, table_of(row)) for row in rows], axis=1)


def columns(head):
    if isinstance(head, int):
        return slice(head * WIDTH, (head + 1) * WIDTH)
    return pl.ds(pl.multiple_of(head * WIDTH, WIDTH), WIDTH)


def bounds(heads, parts):
    rows = heads * WIDTH
    cuts = [rows * n // parts // 8 * 8 for n in range(parts + 1)]
    return list(zip(cuts, cuts[1:]))


def overlaps(cuts, head):
    found = []
    for n, (low, high) in enumerate(cuts):
        start, stop = max(low, head * WIDTH), min(high, (head + 1) * WIDTH)
        if start < stop:
            found.append((n, slice(start - low, stop - low), slice(start, stop)))
    return found


def put_states(outs, cuts, seeds, base, at, k_ref, v_ref):
    size = cuts[0][1]
    outs[0][size:, :] = jnp.zeros((outs[0].shape[0] - size, outs[0].shape[1]), jnp.float32)
    for i in range(cuts[-1][1] // WIDTH):
        fk = features(k_ref[:, columns(at + i)], seeds, base + at + i)
        state = lax.dot_general(
            v_ref[:, columns(at + i)], fk, TN, preferred_element_type=jnp.float32
        )
        for n, rows, whole in overlaps(cuts, i):
            outs[n][rows, :] = state[whole.start - i * WIDTH : whole.stop - i * WIDTH, :]
        outs[0][size + i : size + i + 1, :] = jnp.sum(
            fk.astype(jnp.float32), axis=0, keepdims=True
        )


def state_kernel(singles, cuts, which, places_ref, seeds_hbm, k_hbm, v_hbm, *refs):
    extra, refs = (refs[:1], refs[1:]) if which == 0 else ((), refs)
    half = cuts[-1][1] // WIDTH
    alone = sum(singles)
    outs, refs = refs[: len(singles) + len(cuts)], refs[len(singles) + len(cuts) :]
    gain_ref, refs = (refs[0], refs[1:]) if which == 0 else (None, refs)
    seeds_ref, k_ref, v_ref, kd_ref, vd_ref, sems = refs
    first = first_of(which, half, places_ref)
    span = pl.ds(pl.multiple_of(first * WIDTH, WIDTH), half * WIDTH)
    rest = pl.ds(2 * half * WIDTH, kd_ref.shape[1])
    pairs = [(seeds_hbm, seeds_ref)]
    if alone:
        pairs += [(k_hbm.at[:, rest], kd_ref), (v_hbm.at[:, rest], vd_ref)]
    pairs += [(gain_hbm, gain_ref) for gain_hbm in extra]
    pairs += [(k_hbm.at[:, span], k_ref), (v_hbm.at[:, span], v_ref)]
    copies = [pltpu.make_async_copy(a, b, sems.at[n]) for n, (a, b) in enumerate(pairs)]
    for copy in copies:
        copy.start()
    copies[0].wait()
    seeds = seeds_ref[...].astype(jnp.float32)
    if alone:
        copies[1].wait()
        copies[2].wait()
        at = 0
        for n, size in enumerate(singles):
            put_states([outs[n]], bounds(size, 1), seeds, 2 * half, at, kd_ref, vd_ref)
            at += size
    for copy in copies[3 if alone else 1 :]:
        copy.wait()
    put_states(outs[len(singles) :], cuts, rotated(seeds, first), 0, 0, k_ref, v_ref)


def local_kernel(half, work, places_ref, _, seeds_ref, q_ref, k_ref, v_ref, *outs):
    tok = q_ref.shape[0]
    seeds = seeds_ref[...].astype(jnp.float32)
    rows = lax.broadcasted_iota(jnp.int32, (tok, tok), 0)
    causal = lax.broadcasted_iota(jnp.int32, (tok, tok), 1) <= rows
    for n, (group, i) in enumerate(work):
        num_ref, den_ref, fq_ref = outs[3 * n : 3 * n + 3]
        if group == 2:
            head, mine, i = 2 * half + i, seeds, 2 * half + i
        else:
            first = first_of(group, half, places_ref)
            head, mine = first + i, rotated(seeds, first)
        fk = features(k_ref[:, columns(head)], mine, i)
        fq = features(q_ref[:, columns(head)], mine, i)
        fq_ref[...] = fq
        scores = lax.dot_general(fq, fk, NT, preferred_element_type=jnp.float32)
        scores = jnp.where(causal, scores, 0.0)
        num_ref[...] = jnp.dot(
            scores.astype(jnp.bfloat16),
            v_ref[:, columns(head)],
            preferred_element_type=jnp.float32,
        )
        den_ref[...] = jnp.broadcast_to(jnp.sum(scores, axis=1, keepdims=True), (tok, WIDTH))


def send_kernel(places_ref, _, *refs):
    refs[-1][...] = functools.reduce(lambda a, b: a + b, [ref[...] for ref in refs[:-1]])


def pass_kernel(levels, crossed, places_ref, _, *refs):
    arrived, refs = refs[:levels], refs[levels:]
    own_ref = refs[-1]
    sent_ref, ours = (None, refs[:-1]) if crossed else (refs[-2], refs[:-2])
    prior = jnp.zeros(own_ref.shape, jnp.float32)
    for n, ref in enumerate(arrived):
        level = lax.div(places_ref[0], 2)
        prior = jnp.where(level == n + 1, ref[0 : prior.shape[0], :], prior)
    right = lax.rem(places_ref[0], 2) == 1
    if sent_ref is not None:
        sent_ref[...] = prior + jnp.where(right, 0.0, ours[0][...])
    own_ref[...] = prior + jnp.where(right, ours[1][...], 0.0) if len(ours) > 1 else prior


def join_kernel(half, work, places_ref, _, gain_ref, *refs):
    count = len(work)
    heads_refs, squares_ref = refs[-count - 1 : -1], refs[-1]
    squares = jnp.zeros(heads_refs[0].shape, jnp.float32)
    for (group, i, cuts, n, copies), out_ref in zip(work, heads_refs):
        num_ref, den_ref, fq_ref = refs[:3]
        state, total = 0.0, 0.0
        for _ in range(copies):
            parts = refs[3 : 3 + len(cuts)]
            refs = refs[:3] + refs[3 + len(cuts) :]
            rows = [parts[m][at, :] for m, at, _ in overlaps(cuts, n)]
            state = state + (rows[0] if len(rows) == 1 else jnp.concatenate(rows, axis=0))
            total = total + parts[0][cuts[0][1] + n : cuts[0][1] + n + 1, :]
        refs = refs[3:]
        wide = jnp.concatenate([state, jnp.broadcast_to(total, state.shape)], axis=0)
        upper = wide.astype(jnp.bfloat16)
        lower = (wide - upper.astype(jnp.float32)).astype(jnp.bfloat16)
        fq = fq_ref[...]
        both = lax.dot_general(fq, upper, NT, preferred_element_type=jnp.float32)
        both = both + lax.dot_general(fq, lower, NT, preferred_element_type=jnp.float32)
        head = (num_ref[...] + both[:, :WIDTH]) / (den_ref[...] + both[:, WIDTH:])
        place = 2 * half + i if group == 2 else first_of(group, half, places_ref) + i
        out_ref[...] = head * gain_ref[:, columns(place)]
        squares = squares + head * head
    rows = jnp.broadcast_to(jnp.sum(squares, axis=1, keepdims=True), squares.shape)
    squares_ref[...] = rows.T[0:8, :]
    if len(refs) > count + 1:
        squares_ref[...] += refs[0][...]


def norm_kernel(half, entries, work, places_ref, *refs):
    heads, squares, out_ref = refs[: len(work)], refs[len(work) : -1], refs[-1]
    tok = out_ref.shape[0]
    overall = functools.reduce(lambda a, b: a + b, [ref[...] for ref in squares])
    factor = lax.rsqrt(overall / entries + 1e-06)
    wide = jnp.broadcast_to(factor[0:1, :], (WIDTH, tok)).T
    for (group, i), source in zip(work, heads):
        place = 2 * half + i if group == 2 else first_of(group, half, places_ref) + i
        out_ref[:, columns(place)] = (source[...] * wide).astype(jnp.bfloat16)


def call(kernel, outs, ins, flops, scratch=(), specs=(), place=VMEM, limit=16 * MIB):
    moved = sum(x.size * x.dtype.itemsize for x in ins)
    moved += sum(x.size * jnp.dtype(x.dtype).itemsize for x in jax.tree.leaves(outs))
    return pl.pallas_call(
        kernel,
        out_shape=outs,
        in_specs=[SMEM, *specs] + [place] * (len(ins) - 1 - len(specs)),
        out_specs=jax.tree.map(lambda _: VMEM, outs),
        scratch_shapes=list(scratch),
        compiler_params=pltpu.CompilerParams(vmem_limit_bytes=limit),
        cost_estimate=pl.CostEstimate(flops=flops, bytes_accessed=moved, transcendentals=0),
    )(*ins)


def per_device(queries, keys, values, seeds, gain):
    f32, bf16 = jnp.float32, jnp.bfloat16
    tok = queries.shape[0]
    heads, feats = seeds.shape
    singles = DIRECTS + CROSSES
    alone = sum(singles)
    half = (heads - alone) // 2
    count = lax.axis_size("seq")
    depth = count // 2
    across = lax.axis_size("tp")
    mine = lax.axis_index("seq")
    places = mine.reshape(1)
    shape = lambda *dims, dtype=f32: jax.ShapeDtypeStruct(dims, dtype)
    cuts = bounds(half, PARTS)

    def state_shapes(cuts):
        return [shape(b - a + (8 if a == 0 else 0), feats) for a, b in cuts]

    def states(singles, which, limit):
        part = pltpu.VMEM((tok, half * WIDTH), keys.dtype)
        rest = pltpu.VMEM((tok, max(1, alone) * WIDTH), keys.dtype)
        return call(
            functools.partial(state_kernel, singles, cuts, which),
            [x for size in singles for x in state_shapes(bounds(size, 1))]
            + state_shapes(cuts)
            + ([shape(1, heads * WIDTH)] if which == 0 else []),
            (places, seeds, keys, values, *([gain.reshape(1, -1)] if which == 0 else [])),
            (sum(singles) + half) * tok * feats * WIDTH * 4,
            [pltpu.VMEM(seeds.shape, seeds.dtype), part, part, rest, rest]
            + [pltpu.SemaphoreType.DMA((5,))],
            place=HBM,
            limit=limit,
        )

    swap = [(i, i ^ 1) for i in range(count)]
    first = states(singles, 1, 60 * MIB)
    direct, cross = first[: len(DIRECTS)], first[len(DIRECTS) : len(singles)]
    theirs = first[len(singles) :]
    incoming = [lax.ppermute(part, "seq", swap) for part in [*theirs, *cross]]
    *ours, gain = states((), 0, 40 * MIB)
    chunks = [*[(part,) for part in direct], *zip([*ours, *cross], incoming)]
    total = len(chunks)
    locals_, arrivals, own, passed = {}, {}, [None] * total, [None] * total
    work = [[(2, i) for i in range(alone)][n : n + 2] for n in range(0, alone, 2)]
    work += [[(0, i), (1, i)] for i in range(half)]
    homes = [(n, i) for n, size in enumerate(singles) for i in range(size)]
    last = places

    def hop(stage, i):
        nonlocal last
        parts = chunks[i] if stage == 1 else (arrivals[stage - 1, i], *chunks[i])
        sent = parts[0]
        if len(parts) > 1:
            sent = call(
                send_kernel,
                shape(*sent.shape),
                (places, last, *parts),
                GLUE_COST,
                specs=[ANY],
            )
            last = sent
        pairs = [(2 * stage - 2 + s, 2 * stage + s) for s in range(2)]
        arrivals[stage, i] = lax.ppermute(sent, "seq", pairs)

    def hand(i):
        nonlocal last
        crossed = i >= len(DIRECTS) + PARTS
        like = shape(*chunks[i][0].shape)
        came = [arrivals[z, i] for z in range(1, depth)]
        *sent, own[i] = call(
            functools.partial(pass_kernel, depth - 1, crossed),
            [like] if crossed else [like, like],
            (places, last, *came, *chunks[i]),
            GLUE_COST,
            specs=[ANY],
        )
        last = own[i] if crossed else sent[0]
        if not crossed:
            passed[i] = lax.ppermute(last, "seq", swap)

    def local(piece):
        nonlocal last
        shapes = [shape(tok, WIDTH), shape(tok, WIDTH), shape(tok, feats, dtype=bf16)]
        parts = call(
            functools.partial(local_kernel, half, work[piece]),
            shapes * len(work[piece]),
            (places, last, seeds, queries, keys, values),
            len(work[piece]) * tok * (feats * WIDTH * 4 + tok * (feats + WIDTH) * 2),
            specs=[ANY],
        )
        last = parts[0]
        for n, key in enumerate(work[piece]):
            locals_[key] = parts[3 * n : 3 * n + 3]

    results, squares = {}, None

    def join(todo):
        nonlocal last, squares
        plan, ins = [], []
        for group, i in todo:
            if group == 2:
                n, at = homes[i]
                plan.append((2, i, bounds(singles[n], 1), at, 2 if n < len(DIRECTS) else 1))
                if n < len(DIRECTS):
                    arrays = [own[n], passed[n]]
                else:
                    arrays = [own[n + PARTS]]
            else:
                arrays = (own if group == 0 else passed)[len(DIRECTS) : len(DIRECTS) + PARTS]
                used = max(n for n, _, _ in overlaps(cuts, i)) + 1
                plan.append((group, i, cuts[:used], i, 1))
                arrays = arrays[:used]
            ins += [*locals_[group, i], *arrays]
        *outs, squares = call(
            functools.partial(join_kernel, half, plan),
            [shape(tok, WIDTH)] * len(todo) + [shape(8, tok)],
            (places, last, gain, *ins, *([] if squares is None else [squares])),
            len(todo) * tok * feats * WIDTH * 8,
            specs=[ANY],
        )
        last = squares
        results.update(zip(todo, outs))

    hops = [
        (i + GAP * (stage - 1), stage, i) for stage in range(1, depth + 1) for i in range(total)
    ]
    order = [("X" if stage == depth else stage, i) for _, stage, i in sorted(hops)]
    if ORDER and depth == 4 and total == 5:
        order = ORDER
    singles_done = [(2, i) for i in range(alone)]
    rest = [("L", i) for i in range(len(work))]
    rest += [("J", singles_done), ("J", [(0, i) for i in range(half)])]
    rest += [("J", [(1, i) for i in range(half - 1)]), ("J", [(1, half - 1)])]
    for kind, i in [*order, *rest]:
        if kind == "X":
            hand(i)
        elif kind == "L":
            if work[i][0] not in locals_:
                local(i)
        elif kind == "J":
            if i and i[0] not in results:
                join(i)
        else:
            hop(kind, i)
    gathered = [squares] + [
        lax.ppermute(squares, "tp", [(i, (i ^ k) if across == 4 else (i + k) % across) for i in range(across)])
        for k in range(1, across)
    ]
    return call(
        functools.partial(norm_kernel, half, heads * WIDTH * across, list(results)),
        shape(tok, heads * WIDTH, dtype=bf16),
        (places, *results.values(), *gathered),
        tok * heads * WIDTH * 3,
    )


def solution(mesh):
    placed = (P("seq", "tp"), P("seq", "tp"), P("seq", "tp"), P("tp", None), P("tp"))
    return jax.shard_map(
        per_device, mesh=mesh, in_specs=placed, out_specs=P("seq", "tp"), check_vma=False
    )
```

```python
import functools

import jax
import jax.numpy as jnp
from jax import lax
from jax.experimental import pallas as pl
from jax.experimental.pallas import tpu as pltpu
from jax.sharding import PartitionSpec as P

WIDTH = 128
MIB = 2**20
DIRECTS = (1, 1)
CROSSES = ()
PARTS = 3
GLUE_COST = 10**9
GAP = 2.1
ORDER = [(1, 0), (1, 1), (1, 2), (2, 0), (1, 3), (2, 1), (1, 4), (2, 2), (3, 0), (2, 3), (3, 1), (2, 4), (3, 2), ('X', 0), (3, 3), ('X', 1), (3, 4), ('X', 2), ('L', 0), ('X', 3), ('X', 4), ('L', 1), ('J', [(2, 0), (2, 1)]), ('L', 2), ('L', 3), ('J', [(0, 0), (0, 1), (0, 2)]), ('J', [(1, 0), (1, 1)]), ('J', [(1, 2)])]


NT = (((1,), (1,)), ((), ()))
TN = (((0,), (0,)), ((), ()))
VMEM = pl.BlockSpec(memory_space=pltpu.VMEM)
HBM = pl.BlockSpec(memory_space=pltpu.HBM)
ANY = pl.BlockSpec(memory_space=pl.ANY)
SMEM = pl.BlockSpec(memory_space=pltpu.SMEM)


def first_of(group, half, mine_ref):
    side = lax.rem(mine_ref[0], 2)
    return half * (side if group == 0 else 1 - side)


def rotated(seeds, first):
    heads = seeds.shape[0]
    return pltpu.roll(seeds, lax.rem(heads - first, heads), 0)


def table_of(row):
    square = jnp.broadcast_to(row, (WIDTH, WIDTH))
    return pltpu.roll(square, 0, 1, stride=1, stride_axis=0).astype(jnp.bfloat16)


def phi(x, table):
    mixed = jnp.dot(x, table, preferred_element_type=jnp.float32) * WIDTH ** (-0.25)
    return (jnp.exp(jnp.minimum(mixed, 0.0)) + jnp.maximum(mixed, 0.0)).astype(jnp.bfloat16)


def features(x, seeds, i):
    groups = seeds.shape[1] // WIDTH
    rows = [seeds[i : i + 1, g * WIDTH : (g + 1) * WIDTH] for g in range(groups)]
    return jnp.concatenate([phi(x, table_of(row)) for row in rows], axis=1)


def columns(head):
    if isinstance(head, int):
        return slice(head * WIDTH, (head + 1) * WIDTH)
    return pl.ds(pl.multiple_of(head * WIDTH, WIDTH), WIDTH)


def bounds(heads, parts):
    rows = heads * WIDTH
    cuts = [rows * n // parts // 8 * 8 for n in range(parts + 1)]
    return list(zip(cuts, cuts[1:]))


def overlaps(cuts, head):
    found = []
    for n, (low, high) in enumerate(cuts):
        start, stop = max(low, head * WIDTH), min(high, (head + 1) * WIDTH)
        if start < stop:
            found.append((n, slice(start - low, stop - low), slice(start, stop)))
    return found


def put_states(outs, cuts, seeds, base, at, k_ref, v_ref):
    size = cuts[0][1]
    outs[0][size:, :] = jnp.zeros((outs[0].shape[0] - size, outs[0].shape[1]), jnp.float32)
    for i in range(cuts[-1][1] // WIDTH):
        fk = features(k_ref[:, columns(at + i)], seeds, base + at + i)
        state = lax.dot_general(
            v_ref[:, columns(at + i)], fk, TN, preferred_element_type=jnp.float32
        )
        for n, rows, whole in overlaps(cuts, i):
            outs[n][rows, :] = state[whole.start - i * WIDTH : whole.stop - i * WIDTH, :]
        outs[0][size + i : size + i + 1, :] = jnp.sum(
            fk.astype(jnp.float32), axis=0, keepdims=True
        )


def state_kernel(singles, cuts, which, places_ref, seeds_hbm, k_hbm, v_hbm, *refs):
    extra, refs = (refs[:1], refs[1:]) if which == 0 else ((), refs)
    half = cuts[-1][1] // WIDTH
    alone = sum(singles)
    outs, refs = refs[: len(singles) + len(cuts)], refs[len(singles) + len(cuts) :]
    gain_ref, refs = (refs[0], refs[1:]) if which == 0 else (None, refs)
    seeds_ref, k_ref, v_ref, kd_ref, vd_ref, sems = refs
    first = first_of(which, half, places_ref)
    span = pl.ds(pl.multiple_of(first * WIDTH, WIDTH), half * WIDTH)
    rest = pl.ds(2 * half * WIDTH, kd_ref.shape[1])
    pairs = [(seeds_hbm, seeds_ref)]
    if alone:
        pairs += [(k_hbm.at[:, rest], kd_ref), (v_hbm.at[:, rest], vd_ref)]
    pairs += [(gain_hbm, gain_ref) for gain_hbm in extra]
    pairs += [(k_hbm.at[:, span], k_ref), (v_hbm.at[:, span], v_ref)]
    copies = [pltpu.make_async_copy(a, b, sems.at[n]) for n, (a, b) in enumerate(pairs)]
    for copy in copies:
        copy.start()
    copies[0].wait()
    seeds = seeds_ref[...].astype(jnp.float32)
    if alone:
        copies[1].wait()
        copies[2].wait()
        at = 0
        for n, size in enumerate(singles):
            put_states([outs[n]], bounds(size, 1), seeds, 2 * half, at, kd_ref, vd_ref)
            at += size
    for copy in copies[3 if alone else 1 :]:
        copy.wait()
    put_states(outs[len(singles) :], cuts, rotated(seeds, first), 0, 0, k_ref, v_ref)


def local_kernel(half, work, places_ref, _, seeds_ref, q_ref, k_ref, v_ref, *outs):
    tok = q_ref.shape[0]
    seeds = seeds_ref[...].astype(jnp.float32)
    rows = lax.broadcasted_iota(jnp.int32, (tok, tok), 0)
    causal = lax.broadcasted_iota(jnp.int32, (tok, tok), 1) <= rows
    for n, (group, i) in enumerate(work):
        num_ref, den_ref, fq_ref = outs[3 * n : 3 * n + 3]
        if group == 2:
            head, mine, i = 2 * half + i, seeds, 2 * half + i
        else:
            first = first_of(group, half, places_ref)
            head, mine = first + i, rotated(seeds, first)
        fk = features(k_ref[:, columns(head)], mine, i)
        fq = features(q_ref[:, columns(head)], mine, i)
        fq_ref[...] = fq
        scores = lax.dot_general(fq, fk, NT, preferred_element_type=jnp.float32)
        scores = jnp.where(causal, scores, 0.0)
        num_ref[...] = jnp.dot(
            scores.astype(jnp.bfloat16),
            v_ref[:, columns(head)],
            preferred_element_type=jnp.float32,
        )
        den_ref[...] = jnp.broadcast_to(jnp.sum(scores, axis=1, keepdims=True), (tok, WIDTH))


def send_kernel(places_ref, _, *refs):
    refs[-1][...] = functools.reduce(lambda a, b: a + b, [ref[...] for ref in refs[:-1]])


def pass_kernel(levels, crossed, places_ref, _, *refs):
    arrived, refs = refs[:levels], refs[levels:]
    own_ref = refs[-1]
    sent_ref, ours = (None, refs[:-1]) if crossed else (refs[-2], refs[:-2])
    prior = jnp.zeros(own_ref.shape, jnp.float32)
    for n, ref in enumerate(arrived):
        level = lax.div(places_ref[0], 2)
        prior = jnp.where(level == n + 1, ref[0 : prior.shape[0], :], prior)
    right = lax.rem(places_ref[0], 2) == 1
    if sent_ref is not None:
        sent_ref[...] = prior + jnp.where(right, 0.0, ours[0][...])
    own_ref[...] = prior + jnp.where(right, ours[1][...], 0.0) if len(ours) > 1 else prior


def join_kernel(half, work, final, places_ref, _, gain_ref, *refs):
    count = len(work)
    heads_refs, squares_ref = refs[-count - 1 : -1], refs[-1]
    squares = jnp.zeros(heads_refs[0].shape, jnp.float32)
    for (group, i, cuts, n, copies), out_ref in zip(work, heads_refs):
        num_ref, den_ref, fq_ref = refs[:3]
        state, total = 0.0, 0.0
        for _ in range(copies):
            parts = refs[3 : 3 + len(cuts)]
            refs = refs[:3] + refs[3 + len(cuts) :]
            rows = [parts[m][at, :] for m, at, _ in overlaps(cuts, n)]
            state = state + (rows[0] if len(rows) == 1 else jnp.concatenate(rows, axis=0))
            total = total + parts[0][cuts[0][1] + n : cuts[0][1] + n + 1, :]
        refs = refs[3:]
        wide = jnp.concatenate([state, jnp.broadcast_to(total, state.shape)], axis=0)
        upper = wide.astype(jnp.bfloat16)
        lower = (wide - upper.astype(jnp.float32)).astype(jnp.bfloat16)
        fq = fq_ref[...]
        both = lax.dot_general(fq, upper, NT, preferred_element_type=jnp.float32)
        both = both + lax.dot_general(fq, lower, NT, preferred_element_type=jnp.float32)
        head = (num_ref[...] + both[:, :WIDTH]) / (den_ref[...] + both[:, WIDTH:])
        place = 2 * half + i if group == 2 else first_of(group, half, places_ref) + i
        out_ref[...] = head * gain_ref[:, columns(place)]
        squares = squares + head * head
    if len(refs) > count + 1:
        squares = squares + refs[0][...]
    if final:
        squares = jnp.broadcast_to(jnp.sum(squares, axis=1, keepdims=True), squares.shape).T[0:8, :]
    squares_ref[...] = squares


def norm_kernel(half, entries, work, places_ref, *refs):
    heads, squares, out_ref = refs[: len(work)], refs[len(work) : -1], refs[-1]
    tok = out_ref.shape[0]
    overall = functools.reduce(lambda a, b: a + b, [ref[...] for ref in squares])
    factor = lax.rsqrt(overall / entries + 1e-06)
    wide = jnp.broadcast_to(factor[0:1, :], (WIDTH, tok)).T
    for (group, i), source in zip(work, heads):
        place = 2 * half + i if group == 2 else first_of(group, half, places_ref) + i
        out_ref[:, columns(place)] = (source[...] * wide).astype(jnp.bfloat16)


def call(kernel, outs, ins, flops, scratch=(), specs=(), place=VMEM, limit=16 * MIB):
    moved = sum(x.size * x.dtype.itemsize for x in ins)
    moved += sum(x.size * jnp.dtype(x.dtype).itemsize for x in jax.tree.leaves(outs))
    return pl.pallas_call(
        kernel,
        out_shape=outs,
        in_specs=[SMEM, *specs] + [place] * (len(ins) - 1 - len(specs)),
        out_specs=jax.tree.map(lambda _: VMEM, outs),
        scratch_shapes=list(scratch),
        compiler_params=pltpu.CompilerParams(vmem_limit_bytes=limit),
        cost_estimate=pl.CostEstimate(flops=flops, bytes_accessed=moved, transcendentals=0),
    )(*ins)


def per_device(queries, keys, values, seeds, gain):
    f32, bf16 = jnp.float32, jnp.bfloat16
    tok = queries.shape[0]
    heads, feats = seeds.shape
    singles = DIRECTS + CROSSES
    alone = sum(singles)
    half = (heads - alone) // 2
    count = lax.axis_size("seq")
    depth = count // 2
    across = lax.axis_size("tp")
    mine = lax.axis_index("seq")
    places = mine.reshape(1)
    shape = lambda *dims, dtype=f32: jax.ShapeDtypeStruct(dims, dtype)
    cuts = bounds(half, PARTS)

    def state_shapes(cuts):
        return [shape(b - a + (8 if a == 0 else 0), feats) for a, b in cuts]

    def states(singles, which, limit):
        part = pltpu.VMEM((tok, half * WIDTH), keys.dtype)
        rest = pltpu.VMEM((tok, max(1, alone) * WIDTH), keys.dtype)
        return call(
            functools.partial(state_kernel, singles, cuts, which),
            [x for size in singles for x in state_shapes(bounds(size, 1))]
            + state_shapes(cuts)
            + ([shape(1, heads * WIDTH)] if which == 0 else []),
            (places, seeds, keys, values, *([gain.reshape(1, -1)] if which == 0 else [])),
            (sum(singles) + half) * tok * feats * WIDTH * 4,
            [pltpu.VMEM(seeds.shape, seeds.dtype), part, part, rest, rest]
            + [pltpu.SemaphoreType.DMA((5,))],
            place=HBM,
            limit=limit,
        )

    swap = [(i, i ^ 1) for i in range(count)]
    first = states(singles, 1, 60 * MIB)
    direct, cross = first[: len(DIRECTS)], first[len(DIRECTS) : len(singles)]
    theirs = first[len(singles) :]
    incoming = [lax.ppermute(part, "seq", swap) for part in [*theirs, *cross]]
    *ours, gain = states((), 0, 40 * MIB)
    chunks = [*[(part,) for part in direct], *zip([*ours, *cross], incoming)]
    total = len(chunks)
    locals_, arrivals, own, passed = {}, {}, [None] * total, [None] * total
    work = [[(2, i) for i in range(alone)][n : n + 2] for n in range(0, alone, 2)]
    work += [[(0, i), (1, i)] for i in range(half)]
    homes = [(n, i) for n, size in enumerate(singles) for i in range(size)]
    last = places

    def hop(stage, i):
        nonlocal last
        parts = chunks[i] if stage == 1 else (arrivals[stage - 1, i], *chunks[i])
        sent = parts[0]
        if len(parts) > 1:
            sent = call(
                send_kernel,
                shape(*sent.shape),
                (places, last, *parts),
                GLUE_COST,
                specs=[ANY],
            )
            last = sent
        pairs = [(2 * stage - 2 + s, 2 * stage + s) for s in range(2)]
        arrivals[stage, i] = lax.ppermute(sent, "seq", pairs)

    def hand(i):
        nonlocal last
        crossed = i >= len(DIRECTS) + PARTS
        like = shape(*chunks[i][0].shape)
        came = [arrivals[z, i] for z in range(1, depth)]
        *sent, own[i] = call(
            functools.partial(pass_kernel, depth - 1, crossed),
            [like] if crossed else [like, like],
            (places, last, *came, *chunks[i]),
            GLUE_COST,
            specs=[ANY],
        )
        last = own[i] if crossed else sent[0]
        if not crossed:
            passed[i] = lax.ppermute(last, "seq", swap)

    def local(piece):
        nonlocal last
        shapes = [shape(tok, WIDTH), shape(tok, WIDTH), shape(tok, feats, dtype=bf16)]
        parts = call(
            functools.partial(local_kernel, half, work[piece]),
            shapes * len(work[piece]),
            (places, last, seeds, queries, keys, values),
            len(work[piece]) * tok * (feats * WIDTH * 4 + tok * (feats + WIDTH) * 2),
            specs=[ANY],
        )
        last = parts[0]
        for n, key in enumerate(work[piece]):
            locals_[key] = parts[3 * n : 3 * n + 3]

    results, squares = {}, None

    def join(todo):
        nonlocal last, squares
        final = len(results) + len(todo) == heads
        plan, ins = [], []
        for group, i in todo:
            if group == 2:
                n, at = homes[i]
                plan.append((2, i, bounds(singles[n], 1), at, 2 if n < len(DIRECTS) else 1))
                if n < len(DIRECTS):
                    arrays = [own[n], passed[n]]
                else:
                    arrays = [own[n + PARTS]]
            else:
                arrays = (own if group == 0 else passed)[len(DIRECTS) : len(DIRECTS) + PARTS]
                used = max(n for n, _, _ in overlaps(cuts, i)) + 1
                plan.append((group, i, cuts[:used], i, 1))
                arrays = arrays[:used]
            ins += [*locals_[group, i], *arrays]
        *outs, squares = call(
            functools.partial(join_kernel, half, plan, final),
            [shape(tok, WIDTH)] * len(todo) + [shape(8, tok) if final else shape(tok, WIDTH)],
            (places, last, gain, *ins, *([] if squares is None else [squares])),
            len(todo) * tok * feats * WIDTH * 8,
            specs=[ANY],
        )
        last = squares
        results.update(zip(todo, outs))

    hops = [
        (i + GAP * (stage - 1), stage, i) for stage in range(1, depth + 1) for i in range(total)
    ]
    order = [("X" if stage == depth else stage, i) for _, stage, i in sorted(hops)]
    if ORDER and depth == 4 and total == 5:
        order = ORDER
    singles_done = [(2, i) for i in range(alone)]
    rest = [("L", i) for i in range(len(work))]
    rest += [("J", singles_done), ("J", [(0, i) for i in range(half)])]
    rest += [("J", [(1, i) for i in range(half - 1)]), ("J", [(1, half - 1)])]
    for kind, i in [*order, *rest]:
        if kind == "X":
            hand(i)
        elif kind == "L":
            if work[i][0] not in locals_:
                local(i)
        elif kind == "J":
            if i and i[0] not in results:
                join(i)
        else:
            hop(kind, i)
    gathered = [squares] + [
        lax.ppermute(squares, "tp", [(i, (i ^ k) if across == 4 else (i + k) % across) for i in range(across)])
        for k in range(1, across)
    ]
    return call(
        functools.partial(norm_kernel, half, heads * WIDTH * across, list(results)),
        shape(tok, heads * WIDTH, dtype=bf16),
        (places, *results.values(), *gathered),
        tok * heads * WIDTH * 3,
    )


def solution(mesh):
    placed = (P("seq", "tp"), P("seq", "tp"), P("seq", "tp"), P("tp", None), P("tp"))
    return jax.shard_map(
        per_device, mesh=mesh, in_specs=placed, out_specs=P("seq", "tp"), check_vma=False
    )
```

```python
import functools

import jax
import jax.numpy as jnp
from jax import lax
from jax.experimental import pallas as pl
from jax.experimental.pallas import tpu as pltpu
from jax.sharding import PartitionSpec as P

WIDTH = 128
MIB = 2**20
DIRECTS = (1, 1)
CROSSES = ()
PARTS = 3
GLUE_COST = 10**9
GAP = 2.1
ORDER = [(1, 0), (1, 1), (1, 2), (2, 0), (1, 3), (2, 1), (1, 4), (2, 2), (3, 0), (2, 3), (3, 1), (2, 4), (3, 2), ('X', 0), (3, 3), ('X', 1), (3, 4), ('X', 2), ('L', 0), ('X', 3), ('X', 4), ('L', 1), ('J', [(2, 0), (2, 1)]), ('L', 2), ('L', 3), ('J', [(0, 0), (0, 1), (0, 2)]), ('J', [(1, 0), (1, 1)]), ('J', [(1, 2)])]


NT = (((1,), (1,)), ((), ()))
TN = (((0,), (0,)), ((), ()))
VMEM = pl.BlockSpec(memory_space=pltpu.VMEM)
HBM = pl.BlockSpec(memory_space=pltpu.HBM)
ANY = pl.BlockSpec(memory_space=pl.ANY)
SMEM = pl.BlockSpec(memory_space=pltpu.SMEM)


def first_of(group, half, mine_ref):
    side = lax.rem(mine_ref[0], 2)
    return half * (side if group == 0 else 1 - side)


def rotated(seeds, first):
    heads = seeds.shape[0]
    return pltpu.roll(seeds, lax.rem(heads - first, heads), 0)


def table_of(row):
    square = jnp.broadcast_to(row, (WIDTH, WIDTH))
    return pltpu.roll(square, 0, 1, stride=1, stride_axis=0).astype(jnp.bfloat16)


def phi(x, table):
    mixed = jnp.dot(x, table, preferred_element_type=jnp.float32) * WIDTH ** (-0.25)
    return (jnp.exp(jnp.minimum(mixed, 0.0)) + jnp.maximum(mixed, 0.0)).astype(jnp.bfloat16)


def features(x, seeds, i):
    groups = seeds.shape[1] // WIDTH
    rows = [seeds[i : i + 1, g * WIDTH : (g + 1) * WIDTH] for g in range(groups)]
    return jnp.concatenate([phi(x, table_of(row)) for row in rows], axis=1)


def columns(head):
    if isinstance(head, int):
        return slice(head * WIDTH, (head + 1) * WIDTH)
    return pl.ds(pl.multiple_of(head * WIDTH, WIDTH), WIDTH)


def bounds(heads, parts):
    rows = heads * WIDTH
    cuts = [rows * n // parts // 8 * 8 for n in range(parts + 1)]
    return list(zip(cuts, cuts[1:]))


def overlaps(cuts, head):
    found = []
    for n, (low, high) in enumerate(cuts):
        start, stop = max(low, head * WIDTH), min(high, (head + 1) * WIDTH)
        if start < stop:
            found.append((n, slice(start - low, stop - low), slice(start, stop)))
    return found


def put_states(outs, cuts, seeds, base, at, k_ref, v_ref):
    size = cuts[0][1]
    outs[0][size:, :] = jnp.zeros((outs[0].shape[0] - size, outs[0].shape[1]), jnp.float32)
    heads = range(cuts[-1][1] // WIDTH)
    fks = [features(k_ref[:, columns(at + i)], seeds, base + at + i) for i in heads]
    states = [
        lax.dot_general(v_ref[:, columns(at + i)], fks[i], TN, preferred_element_type=jnp.float32)
        for i in heads
    ]
    sums = [jnp.sum(fk.astype(jnp.float32), axis=0, keepdims=True) for fk in fks]
    for i in heads:
        for n, rows, whole in overlaps(cuts, i):
            outs[n][rows, :] = states[i][whole.start - i * WIDTH : whole.stop - i * WIDTH, :]
        outs[0][size + i : size + i + 1, :] = sums[i]


def state_kernel(singles, cuts, which, places_ref, seeds_hbm, k_hbm, v_hbm, *refs):
    extra, refs = (refs[:1], refs[1:]) if which == 0 else ((), refs)
    half = cuts[-1][1] // WIDTH
    alone = sum(singles)
    outs, refs = refs[: len(singles) + len(cuts)], refs[len(singles) + len(cuts) :]
    gain_ref, refs = (refs[0], refs[1:]) if which == 0 else (None, refs)
    seeds_ref, k_ref, v_ref, kd_ref, vd_ref, sems = refs
    first = first_of(which, half, places_ref)
    span = pl.ds(pl.multiple_of(first * WIDTH, WIDTH), half * WIDTH)
    rest = pl.ds(2 * half * WIDTH, kd_ref.shape[1])
    pairs = [(seeds_hbm, seeds_ref)]
    if alone:
        pairs += [(k_hbm.at[:, rest], kd_ref), (v_hbm.at[:, rest], vd_ref)]
    pairs += [(gain_hbm, gain_ref) for gain_hbm in extra]
    pairs += [(k_hbm.at[:, span], k_ref), (v_hbm.at[:, span], v_ref)]
    copies = [pltpu.make_async_copy(a, b, sems.at[n]) for n, (a, b) in enumerate(pairs)]
    for copy in copies:
        copy.start()
    copies[0].wait()
    seeds = seeds_ref[...].astype(jnp.float32)
    if alone:
        copies[1].wait()
        copies[2].wait()
        at = 0
        for n, size in enumerate(singles):
            put_states([outs[n]], bounds(size, 1), seeds, 2 * half, at, kd_ref, vd_ref)
            at += size
    for copy in copies[3 if alone else 1 :]:
        copy.wait()
    put_states(outs[len(singles) :], cuts, rotated(seeds, first), 0, 0, k_ref, v_ref)


def local_kernel(half, work, places_ref, _, seeds_ref, q_ref, k_ref, v_ref, *outs):
    tok = q_ref.shape[0]
    seeds = seeds_ref[...].astype(jnp.float32)
    rows = lax.broadcasted_iota(jnp.int32, (tok, tok), 0)
    causal = lax.broadcasted_iota(jnp.int32, (tok, tok), 1) <= rows
    places = []
    for group, i in work:
        if group == 2:
            places.append((2 * half + i, seeds, 2 * half + i))
        else:
            first = first_of(group, half, places_ref)
            places.append((first + i, rotated(seeds, first), i))
    fks = [features(k_ref[:, columns(head)], mine, i) for head, mine, i in places]
    fqs = [features(q_ref[:, columns(head)], mine, i) for head, mine, i in places]
    scores = [
        lax.dot_general(fq, fk, NT, preferred_element_type=jnp.float32)
        for fq, fk in zip(fqs, fks)
    ]
    scores = [jnp.where(causal, score, 0.0) for score in scores]
    nums = [
        jnp.dot(
            score.astype(jnp.bfloat16),
            v_ref[:, columns(head)],
            preferred_element_type=jnp.float32,
        )
        for score, (head, _, _) in zip(scores, places)
    ]
    dens = [jnp.sum(score, axis=1, keepdims=True) for score in scores]
    for n in range(len(work)):
        num_ref, den_ref, fq_ref = outs[3 * n : 3 * n + 3]
        fq_ref[...] = fqs[n]
        num_ref[...] = nums[n]
        den_ref[...] = jnp.broadcast_to(dens[n], (tok, WIDTH))


def send_kernel(places_ref, _, *refs):
    refs[-1][...] = functools.reduce(lambda a, b: a + b, [ref[...] for ref in refs[:-1]])


def pass_kernel(levels, crossed, places_ref, _, *refs):
    arrived, refs = refs[:levels], refs[levels:]
    own_ref = refs[-1]
    sent_ref, ours = (None, refs[:-1]) if crossed else (refs[-2], refs[:-2])
    prior = jnp.zeros(own_ref.shape, jnp.float32)
    for n, ref in enumerate(arrived):
        level = lax.div(places_ref[0], 2)
        prior = jnp.where(level == n + 1, ref[0 : prior.shape[0], :], prior)
    right = lax.rem(places_ref[0], 2) == 1
    if sent_ref is not None:
        sent_ref[...] = prior + jnp.where(right, 0.0, ours[0][...])
    own_ref[...] = prior + jnp.where(right, ours[1][...], 0.0) if len(ours) > 1 else prior


def join_kernel(half, work, final, places_ref, _, gain_ref, *refs):
    count = len(work)
    heads_refs, squares_ref = refs[-count - 1 : -1], refs[-1]
    squares = jnp.zeros(heads_refs[0].shape, jnp.float32)
    for (group, i, cuts, n, copies), out_ref in zip(work, heads_refs):
        num_ref, den_ref, fq_ref = refs[:3]
        state, total = 0.0, 0.0
        for _ in range(copies):
            parts = refs[3 : 3 + len(cuts)]
            refs = refs[:3] + refs[3 + len(cuts) :]
            rows = [parts[m][at, :] for m, at, _ in overlaps(cuts, n)]
            state = state + (rows[0] if len(rows) == 1 else jnp.concatenate(rows, axis=0))
            total = total + parts[0][cuts[0][1] + n : cuts[0][1] + n + 1, :]
        refs = refs[3:]
        wide = jnp.concatenate([state, jnp.broadcast_to(total, state.shape)], axis=0)
        upper = wide.astype(jnp.bfloat16)
        lower = (wide - upper.astype(jnp.float32)).astype(jnp.bfloat16)
        fq = fq_ref[...]
        both = lax.dot_general(fq, upper, NT, preferred_element_type=jnp.float32)
        both = both + lax.dot_general(fq, lower, NT, preferred_element_type=jnp.float32)
        head = (num_ref[...] + both[:, :WIDTH]) / (den_ref[...] + both[:, WIDTH:])
        place = 2 * half + i if group == 2 else first_of(group, half, places_ref) + i
        out_ref[...] = head * gain_ref[:, columns(place)]
        squares = squares + head * head
    if len(refs) > count + 1:
        squares = squares + refs[0][...]
    if final:
        squares = jnp.broadcast_to(jnp.sum(squares, axis=1, keepdims=True), squares.shape).T[0:8, :]
    squares_ref[...] = squares


def norm_kernel(half, entries, work, places_ref, *refs):
    heads, squares, out_ref = refs[: len(work)], refs[len(work) : -1], refs[-1]
    tok = out_ref.shape[0]
    overall = functools.reduce(lambda a, b: a + b, [ref[...] for ref in squares])
    factor = lax.rsqrt(overall / entries + 1e-06)
    wide = jnp.broadcast_to(factor[0:1, :], (WIDTH, tok)).T
    for (group, i), source in zip(work, heads):
        place = 2 * half + i if group == 2 else first_of(group, half, places_ref) + i
        out_ref[:, columns(place)] = (source[...] * wide).astype(jnp.bfloat16)


def call(kernel, outs, ins, flops, scratch=(), specs=(), place=VMEM, limit=16 * MIB):
    moved = sum(x.size * x.dtype.itemsize for x in ins)
    moved += sum(x.size * jnp.dtype(x.dtype).itemsize for x in jax.tree.leaves(outs))
    return pl.pallas_call(
        kernel,
        out_shape=outs,
        in_specs=[SMEM, *specs] + [place] * (len(ins) - 1 - len(specs)),
        out_specs=jax.tree.map(lambda _: VMEM, outs),
        scratch_shapes=list(scratch),
        compiler_params=pltpu.CompilerParams(vmem_limit_bytes=limit),
        cost_estimate=pl.CostEstimate(flops=flops, bytes_accessed=moved, transcendentals=0),
    )(*ins)


def per_device(queries, keys, values, seeds, gain):
    f32, bf16 = jnp.float32, jnp.bfloat16
    tok = queries.shape[0]
    heads, feats = seeds.shape
    singles = DIRECTS + CROSSES
    alone = sum(singles)
    half = (heads - alone) // 2
    count = lax.axis_size("seq")
    depth = count // 2
    across = lax.axis_size("tp")
    mine = lax.axis_index("seq")
    places = mine.reshape(1)
    shape = lambda *dims, dtype=f32: jax.ShapeDtypeStruct(dims, dtype)
    cuts = bounds(half, PARTS)

    def state_shapes(cuts):
        return [shape(b - a + (8 if a == 0 else 0), feats) for a, b in cuts]

    def states(singles, which, limit):
        part = pltpu.VMEM((tok, half * WIDTH), keys.dtype)
        rest = pltpu.VMEM((tok, max(1, alone) * WIDTH), keys.dtype)
        return call(
            functools.partial(state_kernel, singles, cuts, which),
            [x for size in singles for x in state_shapes(bounds(size, 1))]
            + state_shapes(cuts)
            + ([shape(1, heads * WIDTH)] if which == 0 else []),
            (places, seeds, keys, values, *([gain.reshape(1, -1)] if which == 0 else [])),
            (sum(singles) + half) * tok * feats * WIDTH * 4,
            [pltpu.VMEM(seeds.shape, seeds.dtype), part, part, rest, rest]
            + [pltpu.SemaphoreType.DMA((5,))],
            place=HBM,
            limit=limit,
        )

    swap = [(i, i ^ 1) for i in range(count)]
    first = states(singles, 1, 60 * MIB)
    direct, cross = first[: len(DIRECTS)], first[len(DIRECTS) : len(singles)]
    theirs = first[len(singles) :]
    incoming = [lax.ppermute(part, "seq", swap) for part in [*theirs, *cross]]
    *ours, gain = states((), 0, 40 * MIB)
    chunks = [*[(part,) for part in direct], *zip([*ours, *cross], incoming)]
    total = len(chunks)
    locals_, arrivals, own, passed = {}, {}, [None] * total, [None] * total
    work = [[(2, i) for i in range(alone)][n : n + 2] for n in range(0, alone, 2)]
    work += [[(0, i), (1, i)] for i in range(half)]
    homes = [(n, i) for n, size in enumerate(singles) for i in range(size)]
    last = places

    def hop(stage, i):
        nonlocal last
        parts = chunks[i] if stage == 1 else (arrivals[stage - 1, i], *chunks[i])
        sent = parts[0]
        if len(parts) > 1:
            sent = call(
                send_kernel,
                shape(*sent.shape),
                (places, last, *parts),
                GLUE_COST,
                specs=[ANY],
            )
            last = sent
        pairs = [(2 * stage - 2 + s, 2 * stage + s) for s in range(2)]
        arrivals[stage, i] = lax.ppermute(sent, "seq", pairs)

    def hand(i):
        nonlocal last
        crossed = i >= len(DIRECTS) + PARTS
        like = shape(*chunks[i][0].shape)
        came = [arrivals[z, i] for z in range(1, depth)]
        *sent, own[i] = call(
            functools.partial(pass_kernel, depth - 1, crossed),
            [like] if crossed else [like, like],
            (places, last, *came, *chunks[i]),
            GLUE_COST,
            specs=[ANY],
        )
        last = own[i] if crossed else sent[0]
        if not crossed:
            passed[i] = lax.ppermute(last, "seq", swap)

    def local(piece):
        nonlocal last
        shapes = [shape(tok, WIDTH), shape(tok, WIDTH), shape(tok, feats, dtype=bf16)]
        parts = call(
            functools.partial(local_kernel, half, work[piece]),
            shapes * len(work[piece]),
            (places, last, seeds, queries, keys, values),
            len(work[piece]) * tok * (feats * WIDTH * 4 + tok * (feats + WIDTH) * 2),
            specs=[ANY],
        )
        last = parts[0]
        for n, key in enumerate(work[piece]):
            locals_[key] = parts[3 * n : 3 * n + 3]

    results, squares = {}, None

    def join(todo):
        nonlocal last, squares
        final = len(results) + len(todo) == heads
        plan, ins = [], []
        for group, i in todo:
            if group == 2:
                n, at = homes[i]
                plan.append((2, i, bounds(singles[n], 1), at, 2 if n < len(DIRECTS) else 1))
                if n < len(DIRECTS):
                    arrays = [own[n], passed[n]]
                else:
                    arrays = [own[n + PARTS]]
            else:
                arrays = (own if group == 0 else passed)[len(DIRECTS) : len(DIRECTS) + PARTS]
                used = max(n for n, _, _ in overlaps(cuts, i)) + 1
                plan.append((group, i, cuts[:used], i, 1))
                arrays = arrays[:used]
            ins += [*locals_[group, i], *arrays]
        *outs, squares = call(
            functools.partial(join_kernel, half, plan, final),
            [shape(tok, WIDTH)] * len(todo) + [shape(8, tok) if final else shape(tok, WIDTH)],
            (places, last, gain, *ins, *([] if squares is None else [squares])),
            len(todo) * tok * feats * WIDTH * 8,
            specs=[ANY],
        )
        last = squares
        results.update(zip(todo, outs))

    hops = [
        (i + GAP * (stage - 1), stage, i) for stage in range(1, depth + 1) for i in range(total)
    ]
    order = [("X" if stage == depth else stage, i) for _, stage, i in sorted(hops)]
    if ORDER and depth == 4 and total == 5:
        order = ORDER
    singles_done = [(2, i) for i in range(alone)]
    rest = [("L", i) for i in range(len(work))]
    rest += [("J", singles_done), ("J", [(0, i) for i in range(half)])]
    rest += [("J", [(1, i) for i in range(half - 1)]), ("J", [(1, half - 1)])]
    for kind, i in [*order, *rest]:
        if kind == "X":
            hand(i)
        elif kind == "L":
            if work[i][0] not in locals_:
                local(i)
        elif kind == "J":
            if i and i[0] not in results:
                join(i)
        else:
            hop(kind, i)
    gathered = [squares] + [
        lax.ppermute(squares, "tp", [(i, (i ^ k) if across == 4 else (i + k) % across) for i in range(across)])
        for k in range(1, across)
    ]
    return call(
        functools.partial(norm_kernel, half, heads * WIDTH * across, list(results)),
        shape(tok, heads * WIDTH, dtype=bf16),
        (places, *results.values(), *gathered),
        tok * heads * WIDTH * 3,
    )


def solution(mesh):
    placed = (P("seq", "tp"), P("seq", "tp"), P("seq", "tp"), P("tp", None), P("tp"))
    return jax.shard_map(
        per_device, mesh=mesh, in_specs=placed, out_specs=P("seq", "tp"), check_vma=False
    )
```

```python
import functools

import jax
import jax.numpy as jnp
from jax import lax
from jax.experimental import pallas as pl
from jax.experimental.pallas import tpu as pltpu
from jax.sharding import PartitionSpec as P

WIDTH = 128
MIB = 2**20
DIRECTS = (1, 1)
CROSSES = ()
PARTS = 3
GLUE_COST = 10**9
GAP = 2.1
ORDER = [(1, 0), (1, 1), (1, 2), (2, 0), (1, 3), (2, 1), (1, 4), (2, 2), (3, 0), (2, 3), (3, 1), (2, 4), (3, 2), ('X', 0), (3, 3), ('X', 1), (3, 4), ('X', 2), ('L', 0), ('X', 3), ('X', 4), ('L', 1), ('J', [(2, 0), (2, 1)]), ('L', 2), ('L', 3), ('J', [(0, 0), (0, 1), (0, 2)]), ('J', [(1, 0), (1, 1)]), ('J', [(1, 2)])]


NT = (((1,), (1,)), ((), ()))
TN = (((0,), (0,)), ((), ()))
VMEM = pl.BlockSpec(memory_space=pltpu.VMEM)
HBM = pl.BlockSpec(memory_space=pltpu.HBM)
ANY = pl.BlockSpec(memory_space=pl.ANY)
SMEM = pl.BlockSpec(memory_space=pltpu.SMEM)


def first_of(group, half, mine_ref):
    side = lax.rem(mine_ref[0], 2)
    return half * (side if group == 0 else 1 - side)


def rotated(seeds, first):
    heads = seeds.shape[0]
    return pltpu.roll(seeds, lax.rem(heads - first, heads), 0)


def table_of(row):
    square = jnp.broadcast_to(row, (WIDTH, WIDTH))
    return pltpu.roll(square, 0, 1, stride=1, stride_axis=0).astype(jnp.bfloat16)


def phi(x, table):
    mixed = jnp.dot(x, table, preferred_element_type=jnp.float32) * WIDTH ** (-0.25)
    return (jnp.exp(jnp.minimum(mixed, 0.0)) + jnp.maximum(mixed, 0.0)).astype(jnp.bfloat16)


def features(x, seeds, i):
    groups = seeds.shape[1] // WIDTH
    rows = [seeds[i : i + 1, g * WIDTH : (g + 1) * WIDTH] for g in range(groups)]
    return jnp.concatenate([phi(x, table_of(row)) for row in rows], axis=1)


def columns(head):
    if isinstance(head, int):
        return slice(head * WIDTH, (head + 1) * WIDTH)
    return pl.ds(pl.multiple_of(head * WIDTH, WIDTH), WIDTH)


def bounds(heads, parts):
    rows = heads * WIDTH
    cuts = [rows * n // parts // 8 * 8 for n in range(parts + 1)]
    return list(zip(cuts, cuts[1:]))


def overlaps(cuts, head):
    found = []
    for n, (low, high) in enumerate(cuts):
        start, stop = max(low, head * WIDTH), min(high, (head + 1) * WIDTH)
        if start < stop:
            found.append((n, slice(start - low, stop - low), slice(start, stop)))
    return found


def put_states(jobs):
    places = [(job, i) for job in jobs for i in range(job[1][-1][1] // WIDTH)]
    fks = [
        features(k_ref[:, columns(at + i)], seeds, base + at + i)
        for (_, _, seeds, base, at, k_ref, _), i in places
    ]
    states = [
        lax.dot_general(v_ref[:, columns(at + i)], fk, TN, preferred_element_type=jnp.float32)
        for ((_, _, _, _, at, _, v_ref), i), fk in zip(places, fks)
    ]
    sums = [jnp.sum(fk.astype(jnp.float32), axis=0, keepdims=True) for fk in fks]
    for ((outs, cuts, *_), i), state, total in zip(places, states, sums):
        size = cuts[0][1]
        if i == 0:
            outs[0][size:, :] = jnp.zeros(
                (outs[0].shape[0] - size, outs[0].shape[1]), jnp.float32
            )
        for n, rows, whole in overlaps(cuts, i):
            outs[n][rows, :] = state[whole.start - i * WIDTH : whole.stop - i * WIDTH, :]
        outs[0][size + i : size + i + 1, :] = total


def state_kernel(singles, cuts, which, places_ref, seeds_hbm, k_hbm, v_hbm, *refs):
    extra, refs = (refs[:1], refs[1:]) if which == 0 else ((), refs)
    half = cuts[-1][1] // WIDTH
    alone = sum(singles)
    outs, refs = refs[: len(singles) + len(cuts)], refs[len(singles) + len(cuts) :]
    gain_ref, refs = (refs[0], refs[1:]) if which == 0 else (None, refs)
    seeds_ref, k_ref, v_ref, kd_ref, vd_ref, sems = refs
    first = first_of(which, half, places_ref)
    span = pl.ds(pl.multiple_of(first * WIDTH, WIDTH), half * WIDTH)
    rest = pl.ds(2 * half * WIDTH, kd_ref.shape[1])
    pairs = [(seeds_hbm, seeds_ref)]
    if alone:
        pairs += [(k_hbm.at[:, rest], kd_ref), (v_hbm.at[:, rest], vd_ref)]
    pairs += [(gain_hbm, gain_ref) for gain_hbm in extra]
    pairs += [(k_hbm.at[:, span], k_ref), (v_hbm.at[:, span], v_ref)]
    copies = [pltpu.make_async_copy(a, b, sems.at[n]) for n, (a, b) in enumerate(pairs)]
    for copy in copies:
        copy.start()
    copies[0].wait()
    seeds = seeds_ref[...].astype(jnp.float32)
    for copy in copies[1:]:
        copy.wait()
    jobs, at = [], 0
    for n, size in enumerate(singles):
        jobs.append(([outs[n]], bounds(size, 1), seeds, 2 * half, at, kd_ref, vd_ref))
        at += size
    jobs.append((outs[len(singles) :], cuts, rotated(seeds, first), 0, 0, k_ref, v_ref))
    put_states(jobs)


def local_kernel(half, work, places_ref, _, seeds_ref, q_ref, k_ref, v_ref, *outs):
    tok = q_ref.shape[0]
    seeds = seeds_ref[...].astype(jnp.float32)
    rows = lax.broadcasted_iota(jnp.int32, (tok, tok), 0)
    causal = lax.broadcasted_iota(jnp.int32, (tok, tok), 1) <= rows
    places = []
    for group, i in work:
        if group == 2:
            places.append((2 * half + i, seeds, 2 * half + i))
        else:
            first = first_of(group, half, places_ref)
            places.append((first + i, rotated(seeds, first), i))
    fks = [features(k_ref[:, columns(head)], mine, i) for head, mine, i in places]
    fqs = [features(q_ref[:, columns(head)], mine, i) for head, mine, i in places]
    scores = [
        lax.dot_general(fq, fk, NT, preferred_element_type=jnp.float32)
        for fq, fk in zip(fqs, fks)
    ]
    scores = [jnp.where(causal, score, 0.0) for score in scores]
    nums = [
        jnp.dot(
            score.astype(jnp.bfloat16),
            v_ref[:, columns(head)],
            preferred_element_type=jnp.float32,
        )
        for score, (head, _, _) in zip(scores, places)
    ]
    dens = [jnp.sum(score, axis=1, keepdims=True) for score in scores]
    for n in range(len(work)):
        num_ref, den_ref, fq_ref = outs[3 * n : 3 * n + 3]
        fq_ref[...] = fqs[n]
        num_ref[...] = nums[n]
        den_ref[...] = jnp.broadcast_to(dens[n], (tok, WIDTH))


def send_kernel(places_ref, _, *refs):
    refs[-1][...] = functools.reduce(lambda a, b: a + b, [ref[...] for ref in refs[:-1]])


def pass_kernel(levels, crossed, places_ref, _, *refs):
    arrived, refs = refs[:levels], refs[levels:]
    own_ref = refs[-1]
    sent_ref, ours = (None, refs[:-1]) if crossed else (refs[-2], refs[:-2])
    prior = jnp.zeros(own_ref.shape, jnp.float32)
    for n, ref in enumerate(arrived):
        level = lax.div(places_ref[0], 2)
        prior = jnp.where(level == n + 1, ref[0 : prior.shape[0], :], prior)
    right = lax.rem(places_ref[0], 2) == 1
    if sent_ref is not None:
        sent_ref[...] = prior + jnp.where(right, 0.0, ours[0][...])
    own_ref[...] = prior + jnp.where(right, ours[1][...], 0.0) if len(ours) > 1 else prior


def join_kernel(half, work, final, places_ref, _, gain_ref, *refs):
    count = len(work)
    heads_refs, squares_ref = refs[-count - 1 : -1], refs[-1]
    squares = jnp.zeros(heads_refs[0].shape, jnp.float32)
    for (group, i, cuts, n, copies), out_ref in zip(work, heads_refs):
        num_ref, den_ref, fq_ref = refs[:3]
        state, total = 0.0, 0.0
        for _ in range(copies):
            parts = refs[3 : 3 + len(cuts)]
            refs = refs[:3] + refs[3 + len(cuts) :]
            rows = [parts[m][at, :] for m, at, _ in overlaps(cuts, n)]
            state = state + (rows[0] if len(rows) == 1 else jnp.concatenate(rows, axis=0))
            total = total + parts[0][cuts[0][1] + n : cuts[0][1] + n + 1, :]
        refs = refs[3:]
        wide = jnp.concatenate([state, jnp.broadcast_to(total, state.shape)], axis=0)
        upper = wide.astype(jnp.bfloat16)
        lower = (wide - upper.astype(jnp.float32)).astype(jnp.bfloat16)
        fq = fq_ref[...]
        both = lax.dot_general(fq, upper, NT, preferred_element_type=jnp.float32)
        both = both + lax.dot_general(fq, lower, NT, preferred_element_type=jnp.float32)
        head = (num_ref[...] + both[:, :WIDTH]) / (den_ref[...] + both[:, WIDTH:])
        place = 2 * half + i if group == 2 else first_of(group, half, places_ref) + i
        out_ref[...] = head * gain_ref[:, columns(place)]
        squares = squares + head * head
    if len(refs) > count + 1:
        squares = squares + refs[0][...]
    if final:
        squares = jnp.broadcast_to(jnp.sum(squares, axis=1, keepdims=True), squares.shape).T[0:8, :]
    squares_ref[...] = squares


def norm_kernel(half, entries, work, places_ref, *refs):
    heads, squares, out_ref = refs[: len(work)], refs[len(work) : -1], refs[-1]
    tok = out_ref.shape[0]
    overall = functools.reduce(lambda a, b: a + b, [ref[...] for ref in squares])
    factor = lax.rsqrt(overall / entries + 1e-06)
    wide = jnp.broadcast_to(factor[0:1, :], (WIDTH, tok)).T
    for (group, i), source in zip(work, heads):
        place = 2 * half + i if group == 2 else first_of(group, half, places_ref) + i
        out_ref[:, columns(place)] = (source[...] * wide).astype(jnp.bfloat16)


def call(kernel, outs, ins, flops, scratch=(), specs=(), place=VMEM, limit=16 * MIB):
    moved = sum(x.size * x.dtype.itemsize for x in ins)
    moved += sum(x.size * jnp.dtype(x.dtype).itemsize for x in jax.tree.leaves(outs))
    return pl.pallas_call(
        kernel,
        out_shape=outs,
        in_specs=[SMEM, *specs] + [place] * (len(ins) - 1 - len(specs)),
        out_specs=jax.tree.map(lambda _: VMEM, outs),
        scratch_shapes=list(scratch),
        compiler_params=pltpu.CompilerParams(vmem_limit_bytes=limit),
        cost_estimate=pl.CostEstimate(flops=flops, bytes_accessed=moved, transcendentals=0),
    )(*ins)


def per_device(queries, keys, values, seeds, gain):
    f32, bf16 = jnp.float32, jnp.bfloat16
    tok = queries.shape[0]
    heads, feats = seeds.shape
    singles = DIRECTS + CROSSES
    alone = sum(singles)
    half = (heads - alone) // 2
    count = lax.axis_size("seq")
    depth = count // 2
    across = lax.axis_size("tp")
    mine = lax.axis_index("seq")
    places = mine.reshape(1)
    shape = lambda *dims, dtype=f32: jax.ShapeDtypeStruct(dims, dtype)
    cuts = bounds(half, PARTS)

    def state_shapes(cuts):
        return [shape(b - a + (8 if a == 0 else 0), feats) for a, b in cuts]

    def states(singles, which, limit):
        part = pltpu.VMEM((tok, half * WIDTH), keys.dtype)
        rest = pltpu.VMEM((tok, max(1, alone) * WIDTH), keys.dtype)
        return call(
            functools.partial(state_kernel, singles, cuts, which),
            [x for size in singles for x in state_shapes(bounds(size, 1))]
            + state_shapes(cuts)
            + ([shape(1, heads * WIDTH)] if which == 0 else []),
            (places, seeds, keys, values, *([gain.reshape(1, -1)] if which == 0 else [])),
            (sum(singles) + half) * tok * feats * WIDTH * 4,
            [pltpu.VMEM(seeds.shape, seeds.dtype), part, part, rest, rest]
            + [pltpu.SemaphoreType.DMA((5,))],
            place=HBM,
            limit=limit,
        )

    swap = [(i, i ^ 1) for i in range(count)]
    first = states(singles, 1, 60 * MIB)
    direct, cross = first[: len(DIRECTS)], first[len(DIRECTS) : len(singles)]
    theirs = first[len(singles) :]
    incoming = [lax.ppermute(part, "seq", swap) for part in [*theirs, *cross]]
    *ours, gain = states((), 0, 40 * MIB)
    chunks = [*[(part,) for part in direct], *zip([*ours, *cross], incoming)]
    total = len(chunks)
    locals_, arrivals, own, passed = {}, {}, [None] * total, [None] * total
    work = [[(2, i) for i in range(alone)][n : n + 2] for n in range(0, alone, 2)]
    work += [[(0, i), (1, i)] for i in range(half)]
    homes = [(n, i) for n, size in enumerate(singles) for i in range(size)]
    last = places

    def hop(stage, i):
        nonlocal last
        parts = chunks[i] if stage == 1 else (arrivals[stage - 1, i], *chunks[i])
        sent = parts[0]
        if len(parts) > 1:
            sent = call(
                send_kernel,
                shape(*sent.shape),
                (places, last, *parts),
                GLUE_COST,
                specs=[ANY],
            )
            last = sent
        pairs = [(2 * stage - 2 + s, 2 * stage + s) for s in range(2)]
        arrivals[stage, i] = lax.ppermute(sent, "seq", pairs)

    def hand(i):
        nonlocal last
        crossed = i >= len(DIRECTS) + PARTS
        like = shape(*chunks[i][0].shape)
        came = [arrivals[z, i] for z in range(1, depth)]
        *sent, own[i] = call(
            functools.partial(pass_kernel, depth - 1, crossed),
            [like] if crossed else [like, like],
            (places, last, *came, *chunks[i]),
            GLUE_COST,
            specs=[ANY],
        )
        last = own[i] if crossed else sent[0]
        if not crossed:
            passed[i] = lax.ppermute(last, "seq", swap)

    def local(piece):
        nonlocal last
        shapes = [shape(tok, WIDTH), shape(tok, WIDTH), shape(tok, feats, dtype=bf16)]
        parts = call(
            functools.partial(local_kernel, half, work[piece]),
            shapes * len(work[piece]),
            (places, last, seeds, queries, keys, values),
            len(work[piece]) * tok * (feats * WIDTH * 4 + tok * (feats + WIDTH) * 2),
            specs=[ANY],
        )
        last = parts[0]
        for n, key in enumerate(work[piece]):
            locals_[key] = parts[3 * n : 3 * n + 3]

    results, squares = {}, None

    def join(todo):
        nonlocal last, squares
        final = len(results) + len(todo) == heads
        plan, ins = [], []
        for group, i in todo:
            if group == 2:
                n, at = homes[i]
                plan.append((2, i, bounds(singles[n], 1), at, 2 if n < len(DIRECTS) else 1))
                if n < len(DIRECTS):
                    arrays = [own[n], passed[n]]
                else:
                    arrays = [own[n + PARTS]]
            else:
                arrays = (own if group == 0 else passed)[len(DIRECTS) : len(DIRECTS) + PARTS]
                used = max(n for n, _, _ in overlaps(cuts, i)) + 1
                plan.append((group, i, cuts[:used], i, 1))
                arrays = arrays[:used]
            ins += [*locals_[group, i], *arrays]
        *outs, squares = call(
            functools.partial(join_kernel, half, plan, final),
            [shape(tok, WIDTH)] * len(todo) + [shape(8, tok) if final else shape(tok, WIDTH)],
            (places, last, gain, *ins, *([] if squares is None else [squares])),
            len(todo) * tok * feats * WIDTH * 8,
            specs=[ANY],
        )
        last = squares
        results.update(zip(todo, outs))

    hops = [
        (i + GAP * (stage - 1), stage, i) for stage in range(1, depth + 1) for i in range(total)
    ]
    order = [("X" if stage == depth else stage, i) for _, stage, i in sorted(hops)]
    if ORDER and depth == 4 and total == 5:
        order = ORDER
    singles_done = [(2, i) for i in range(alone)]
    rest = [("L", i) for i in range(len(work))]
    rest += [("J", singles_done), ("J", [(0, i) for i in range(half)])]
    rest += [("J", [(1, i) for i in range(half - 1)]), ("J", [(1, half - 1)])]
    for kind, i in [*order, *rest]:
        if kind == "X":
            hand(i)
        elif kind == "L":
            if work[i][0] not in locals_:
                local(i)
        elif kind == "J":
            if i and i[0] not in results:
                join(i)
        else:
            hop(kind, i)
    gathered = [squares] + [
        lax.ppermute(squares, "tp", [(i, (i ^ k) if across == 4 else (i + k) % across) for i in range(across)])
        for k in range(1, across)
    ]
    return call(
        functools.partial(norm_kernel, half, heads * WIDTH * across, list(results)),
        shape(tok, heads * WIDTH, dtype=bf16),
        (places, *results.values(), *gathered),
        tok * heads * WIDTH * 3,
    )


def solution(mesh):
    placed = (P("seq", "tp"), P("seq", "tp"), P("seq", "tp"), P("tp", None), P("tp"))
    return jax.shard_map(
        per_device, mesh=mesh, in_specs=placed, out_specs=P("seq", "tp"), check_vma=False
    )
```

```python
import functools

import jax
import jax.numpy as jnp
from jax import lax
from jax.experimental import pallas as pl
from jax.experimental.pallas import tpu as pltpu
from jax.sharding import PartitionSpec as P

WIDTH = 128
MIB = 2**20
DIRECTS = (1, 1)
CROSSES = ()
PARTS = 3
GLUE_COST = 10**9
GAP = 2.1
ORDER = [(1, 0), (1, 1), ('L', 0), (1, 2), (2, 0), (1, 3), (2, 1), (1, 4), (2, 2), (3, 0), (2, 3), (3, 1), (2, 4), (3, 2), ('X', 0), (3, 3), ('X', 1), (3, 4), ('X', 2), ('X', 3), ('X', 4), ('L', 1), ('J', [(2, 0), (2, 1)]), ('L', 2), ('L', 3), ('J', [(0, 0), (0, 1), (0, 2)]), ('J', [(1, 0), (1, 1)]), ('J', [(1, 2)])]


NT = (((1,), (1,)), ((), ()))
TN = (((0,), (0,)), ((), ()))
VMEM = pl.BlockSpec(memory_space=pltpu.VMEM)
HBM = pl.BlockSpec(memory_space=pltpu.HBM)
ANY = pl.BlockSpec(memory_space=pl.ANY)
SMEM = pl.BlockSpec(memory_space=pltpu.SMEM)


def first_of(group, half, mine_ref):
    side = lax.rem(mine_ref[0], 2)
    return half * (side if group == 0 else 1 - side)


def rotated(seeds, first):
    heads = seeds.shape[0]
    return pltpu.roll(seeds, lax.rem(heads - first, heads), 0)


def table_of(row):
    square = jnp.broadcast_to(row, (WIDTH, WIDTH))
    return pltpu.roll(square, 0, 1, stride=1, stride_axis=0).astype(jnp.bfloat16)


def phi(x, table):
    mixed = jnp.dot(x, table, preferred_element_type=jnp.float32) * WIDTH ** (-0.25)
    return (jnp.exp(jnp.minimum(mixed, 0.0)) + jnp.maximum(mixed, 0.0)).astype(jnp.bfloat16)


def features(x, seeds, i):
    groups = seeds.shape[1] // WIDTH
    rows = [seeds[i : i + 1, g * WIDTH : (g + 1) * WIDTH] for g in range(groups)]
    return jnp.concatenate([phi(x, table_of(row)) for row in rows], axis=1)


def columns(head):
    if isinstance(head, int):
        return slice(head * WIDTH, (head + 1) * WIDTH)
    return pl.ds(pl.multiple_of(head * WIDTH, WIDTH), WIDTH)


def bounds(heads, parts):
    rows = heads * WIDTH
    cuts = [rows * n // parts // 8 * 8 for n in range(parts + 1)]
    return list(zip(cuts, cuts[1:]))


def overlaps(cuts, head):
    found = []
    for n, (low, high) in enumerate(cuts):
        start, stop = max(low, head * WIDTH), min(high, (head + 1) * WIDTH)
        if start < stop:
            found.append((n, slice(start - low, stop - low), slice(start, stop)))
    return found


def put_states(jobs):
    places = [(job, i) for job in jobs for i in range(job[1][-1][1] // WIDTH)]
    fks = [
        features(k_ref[:, columns(at + i)], seeds, base + at + i)
        for (_, _, seeds, base, at, k_ref, _), i in places
    ]
    states = [
        lax.dot_general(v_ref[:, columns(at + i)], fk, TN, preferred_element_type=jnp.float32)
        for ((_, _, _, _, at, _, v_ref), i), fk in zip(places, fks)
    ]
    sums = [jnp.sum(fk.astype(jnp.float32), axis=0, keepdims=True) for fk in fks]
    for ((outs, cuts, *_), i), state, total in zip(places, states, sums):
        size = cuts[0][1]
        if i == 0:
            outs[0][size:, :] = jnp.zeros(
                (outs[0].shape[0] - size, outs[0].shape[1]), jnp.float32
            )
        for n, rows, whole in overlaps(cuts, i):
            outs[n][rows, :] = state[whole.start - i * WIDTH : whole.stop - i * WIDTH, :]
        outs[0][size + i : size + i + 1, :] = total


def state_kernel(singles, cuts, which, places_ref, seeds_hbm, k_hbm, v_hbm, *refs):
    extra, refs = (refs[:1], refs[1:]) if which == 0 else ((), refs)
    half = cuts[-1][1] // WIDTH
    alone = sum(singles)
    outs, refs = refs[: len(singles) + len(cuts)], refs[len(singles) + len(cuts) :]
    gain_ref, refs = (refs[0], refs[1:]) if which == 0 else (None, refs)
    seeds_ref, k_ref, v_ref, kd_ref, vd_ref, sems = refs
    first = first_of(which, half, places_ref)
    span = pl.ds(pl.multiple_of(first * WIDTH, WIDTH), half * WIDTH)
    rest = pl.ds(2 * half * WIDTH, kd_ref.shape[1])
    pairs = [(seeds_hbm, seeds_ref)]
    if alone:
        pairs += [(k_hbm.at[:, rest], kd_ref), (v_hbm.at[:, rest], vd_ref)]
    pairs += [(gain_hbm, gain_ref) for gain_hbm in extra]
    pairs += [(k_hbm.at[:, span], k_ref), (v_hbm.at[:, span], v_ref)]
    copies = [pltpu.make_async_copy(a, b, sems.at[n]) for n, (a, b) in enumerate(pairs)]
    for copy in copies:
        copy.start()
    copies[0].wait()
    seeds = seeds_ref[...].astype(jnp.float32)
    for copy in copies[1:]:
        copy.wait()
    jobs, at = [], 0
    for n, size in enumerate(singles):
        jobs.append(([outs[n]], bounds(size, 1), seeds, 2 * half, at, kd_ref, vd_ref))
        at += size
    jobs.append((outs[len(singles) :], cuts, rotated(seeds, first), 0, 0, k_ref, v_ref))
    put_states(jobs)


def local_kernel(half, work, places_ref, _, seeds_ref, q_ref, k_ref, v_ref, *outs):
    tok = q_ref.shape[0]
    seeds = seeds_ref[...].astype(jnp.float32)
    rows = lax.broadcasted_iota(jnp.int32, (tok, tok), 0)
    causal = lax.broadcasted_iota(jnp.int32, (tok, tok), 1) <= rows
    places = []
    for group, i in work:
        if group == 2:
            places.append((2 * half + i, seeds, 2 * half + i))
        else:
            first = first_of(group, half, places_ref)
            places.append((first + i, rotated(seeds, first), i))
    fks = [features(k_ref[:, columns(head)], mine, i) for head, mine, i in places]
    fqs = [features(q_ref[:, columns(head)], mine, i) for head, mine, i in places]
    scores = [
        lax.dot_general(fq, fk, NT, preferred_element_type=jnp.float32)
        for fq, fk in zip(fqs, fks)
    ]
    scores = [jnp.where(causal, score, 0.0) for score in scores]
    nums = [
        jnp.dot(
            score.astype(jnp.bfloat16),
            v_ref[:, columns(head)],
            preferred_element_type=jnp.float32,
        )
        for score, (head, _, _) in zip(scores, places)
    ]
    dens = [jnp.sum(score, axis=1, keepdims=True) for score in scores]
    for n in range(len(work)):
        num_ref, den_ref, fq_ref = outs[3 * n : 3 * n + 3]
        fq_ref[...] = fqs[n]
        num_ref[...] = nums[n]
        den_ref[...] = jnp.broadcast_to(dens[n], (tok, WIDTH))


def send_kernel(places_ref, _, *refs):
    refs[-1][...] = functools.reduce(lambda a, b: a + b, [ref[...] for ref in refs[:-1]])


def pass_kernel(levels, crossed, places_ref, _, *refs):
    arrived, refs = refs[:levels], refs[levels:]
    own_ref = refs[-1]
    sent_ref, ours = (None, refs[:-1]) if crossed else (refs[-2], refs[:-2])
    prior = jnp.zeros(own_ref.shape, jnp.float32)
    for n, ref in enumerate(arrived):
        level = lax.div(places_ref[0], 2)
        prior = jnp.where(level == n + 1, ref[0 : prior.shape[0], :], prior)
    right = lax.rem(places_ref[0], 2) == 1
    if sent_ref is not None:
        sent_ref[...] = prior + jnp.where(right, 0.0, ours[0][...])
    own_ref[...] = prior + jnp.where(right, ours[1][...], 0.0) if len(ours) > 1 else prior


def join_kernel(half, work, final, places_ref, _, gain_ref, *refs):
    count = len(work)
    heads_refs, squares_ref = refs[-count - 1 : -1], refs[-1]
    wides, locals_ = [], []
    for _, _, cuts, n, copies in work:
        locals_.append(refs[:3])
        state, total = 0.0, 0.0
        refs = refs[3:]
        for _ in range(copies):
            parts, refs = refs[: len(cuts)], refs[len(cuts) :]
            rows = [parts[m][at, :] for m, at, _ in overlaps(cuts, n)]
            state = state + (rows[0] if len(rows) == 1 else jnp.concatenate(rows, axis=0))
            total = total + parts[0][cuts[0][1] + n : cuts[0][1] + n + 1, :]
        wides.append(jnp.concatenate([state, jnp.broadcast_to(total, state.shape)], axis=0))
    uppers = [wide.astype(jnp.bfloat16) for wide in wides]
    lowers = [
        (wide - upper.astype(jnp.float32)).astype(jnp.bfloat16)
        for wide, upper in zip(wides, uppers)
    ]
    fqs = [local[2][...] for local in locals_]
    boths = [
        lax.dot_general(fq, upper, NT, preferred_element_type=jnp.float32)
        + lax.dot_general(fq, lower, NT, preferred_element_type=jnp.float32)
        for fq, upper, lower in zip(fqs, uppers, lowers)
    ]
    heads = [
        (num_ref[...] + both[:, :WIDTH]) / (den_ref[...] + both[:, WIDTH:])
        for (num_ref, den_ref, _), both in zip(locals_, boths)
    ]
    squares = functools.reduce(lambda a, b: a + b, [head * head for head in heads])
    for (group, i, *_), out_ref, head in zip(work, heads_refs, heads):
        place = 2 * half + i if group == 2 else first_of(group, half, places_ref) + i
        out_ref[...] = head * gain_ref[:, columns(place)]
    if len(refs) > count + 1:
        squares = squares + refs[0][...]
    if final:
        squares = jnp.broadcast_to(jnp.sum(squares, axis=1, keepdims=True), squares.shape).T[0:8, :]
    squares_ref[...] = squares


def norm_kernel(half, entries, work, places_ref, *refs):
    heads, squares, out_ref = refs[: len(work)], refs[len(work) : -1], refs[-1]
    tok = out_ref.shape[0]
    overall = functools.reduce(lambda a, b: a + b, [ref[...] for ref in squares])
    factor = lax.rsqrt(overall / entries + 1e-06)
    wide = jnp.broadcast_to(factor[0:1, :], (WIDTH, tok)).T
    for (group, i), source in zip(work, heads):
        place = 2 * half + i if group == 2 else first_of(group, half, places_ref) + i
        out_ref[:, columns(place)] = (source[...] * wide).astype(jnp.bfloat16)


def call(kernel, outs, ins, flops, scratch=(), specs=(), place=VMEM, limit=16 * MIB):
    moved = sum(x.size * x.dtype.itemsize for x in ins)
    moved += sum(x.size * jnp.dtype(x.dtype).itemsize for x in jax.tree.leaves(outs))
    return pl.pallas_call(
        kernel,
        out_shape=outs,
        in_specs=[SMEM, *specs] + [place] * (len(ins) - 1 - len(specs)),
        out_specs=jax.tree.map(lambda _: VMEM, outs),
        scratch_shapes=list(scratch),
        compiler_params=pltpu.CompilerParams(vmem_limit_bytes=limit),
        cost_estimate=pl.CostEstimate(flops=flops, bytes_accessed=moved, transcendentals=0),
    )(*ins)


def per_device(queries, keys, values, seeds, gain):
    f32, bf16 = jnp.float32, jnp.bfloat16
    tok = queries.shape[0]
    heads, feats = seeds.shape
    singles = DIRECTS + CROSSES
    alone = sum(singles)
    half = (heads - alone) // 2
    count = lax.axis_size("seq")
    depth = count // 2
    across = lax.axis_size("tp")
    mine = lax.axis_index("seq")
    places = mine.reshape(1)
    shape = lambda *dims, dtype=f32: jax.ShapeDtypeStruct(dims, dtype)
    cuts = bounds(half, PARTS)

    def state_shapes(cuts):
        return [shape(b - a + (8 if a == 0 else 0), feats) for a, b in cuts]

    def states(singles, which, limit):
        part = pltpu.VMEM((tok, half * WIDTH), keys.dtype)
        rest = pltpu.VMEM((tok, max(1, alone) * WIDTH), keys.dtype)
        return call(
            functools.partial(state_kernel, singles, cuts, which),
            [x for size in singles for x in state_shapes(bounds(size, 1))]
            + state_shapes(cuts)
            + ([shape(1, heads * WIDTH)] if which == 0 else []),
            (places, seeds, keys, values, *([gain.reshape(1, -1)] if which == 0 else [])),
            (sum(singles) + half) * tok * feats * WIDTH * 4,
            [pltpu.VMEM(seeds.shape, seeds.dtype), part, part, rest, rest]
            + [pltpu.SemaphoreType.DMA((5,))],
            place=HBM,
            limit=limit,
        )

    swap = [(i, i ^ 1) for i in range(count)]
    first = states(singles, 1, 60 * MIB)
    direct, cross = first[: len(DIRECTS)], first[len(DIRECTS) : len(singles)]
    theirs = first[len(singles) :]
    incoming = [lax.ppermute(part, "seq", swap) for part in [*theirs, *cross]]
    *ours, gain = states((), 0, 40 * MIB)
    chunks = [*[(part,) for part in direct], *zip([*ours, *cross], incoming)]
    total = len(chunks)
    locals_, arrivals, own, passed = {}, {}, [None] * total, [None] * total
    work = [[(2, i) for i in range(alone)][n : n + 2] for n in range(0, alone, 2)]
    work += [[(0, i), (1, i)] for i in range(half)]
    homes = [(n, i) for n, size in enumerate(singles) for i in range(size)]
    last = places

    def hop(stage, i):
        nonlocal last
        parts = chunks[i] if stage == 1 else (arrivals[stage - 1, i], *chunks[i])
        sent = parts[0]
        if len(parts) > 1:
            sent = call(
                send_kernel,
                shape(*sent.shape),
                (places, last, *parts),
                GLUE_COST,
                specs=[ANY],
            )
            last = sent
        pairs = [(2 * stage - 2 + s, 2 * stage + s) for s in range(2)]
        arrivals[stage, i] = lax.ppermute(sent, "seq", pairs)

    def hand(i):
        nonlocal last
        crossed = i >= len(DIRECTS) + PARTS
        like = shape(*chunks[i][0].shape)
        came = [arrivals[z, i] for z in range(1, depth)]
        *sent, own[i] = call(
            functools.partial(pass_kernel, depth - 1, crossed),
            [like] if crossed else [like, like],
            (places, last, *came, *chunks[i]),
            GLUE_COST,
            specs=[ANY],
        )
        last = own[i] if crossed else sent[0]
        if not crossed:
            passed[i] = lax.ppermute(last, "seq", swap)

    def local(piece):
        nonlocal last
        shapes = [shape(tok, WIDTH), shape(tok, WIDTH), shape(tok, feats, dtype=bf16)]
        parts = call(
            functools.partial(local_kernel, half, work[piece]),
            shapes * len(work[piece]),
            (places, last, seeds, queries, keys, values),
            len(work[piece]) * tok * (feats * WIDTH * 4 + tok * (feats + WIDTH) * 2),
            specs=[ANY],
        )
        last = parts[0]
        for n, key in enumerate(work[piece]):
            locals_[key] = parts[3 * n : 3 * n + 3]

    results, squares = {}, None

    def join(todo):
        nonlocal last, squares
        final = len(results) + len(todo) == heads
        plan, ins = [], []
        for group, i in todo:
            if group == 2:
                n, at = homes[i]
                plan.append((2, i, bounds(singles[n], 1), at, 2 if n < len(DIRECTS) else 1))
                if n < len(DIRECTS):
                    arrays = [own[n], passed[n]]
                else:
                    arrays = [own[n + PARTS]]
            else:
                arrays = (own if group == 0 else passed)[len(DIRECTS) : len(DIRECTS) + PARTS]
                used = max(n for n, _, _ in overlaps(cuts, i)) + 1
                plan.append((group, i, cuts[:used], i, 1))
                arrays = arrays[:used]
            ins += [*locals_[group, i], *arrays]
        *outs, squares = call(
            functools.partial(join_kernel, half, plan, final),
            [shape(tok, WIDTH)] * len(todo) + [shape(8, tok) if final else shape(tok, WIDTH)],
            (places, last, gain, *ins, *([] if squares is None else [squares])),
            len(todo) * tok * feats * WIDTH * 8,
            specs=[ANY],
        )
        last = squares
        results.update(zip(todo, outs))

    hops = [
        (i + GAP * (stage - 1), stage, i) for stage in range(1, depth + 1) for i in range(total)
    ]
    order = [("X" if stage == depth else stage, i) for _, stage, i in sorted(hops)]
    if ORDER and depth == 4 and total == 5:
        order = ORDER
    singles_done = [(2, i) for i in range(alone)]
    rest = [("L", i) for i in range(len(work))]
    rest += [("J", singles_done), ("J", [(0, i) for i in range(half)])]
    rest += [("J", [(1, i) for i in range(half - 1)]), ("J", [(1, half - 1)])]
    for kind, i in [*order, *rest]:
        if kind == "X":
            hand(i)
        elif kind == "L":
            if work[i][0] not in locals_:
                local(i)
        elif kind == "J":
            if i and i[0] not in results:
                join(i)
        else:
            hop(kind, i)
    gathered = [squares] + [
        lax.ppermute(squares, "tp", [(i, (i ^ k) if across == 4 else (i + k) % across) for i in range(across)])
        for k in range(1, across)
    ]
    return call(
        functools.partial(norm_kernel, half, heads * WIDTH * across, list(results)),
        shape(tok, heads * WIDTH, dtype=bf16),
        (places, *results.values(), *gathered),
        tok * heads * WIDTH * 3,
    )


def solution(mesh):
    placed = (P("seq", "tp"), P("seq", "tp"), P("seq", "tp"), P("tp", None), P("tp"))
    return jax.shard_map(
        per_device, mesh=mesh, in_specs=placed, out_specs=P("seq", "tp"), check_vma=False
    )
```

```python
import functools

import jax
import jax.numpy as jnp
from jax import lax
from jax.experimental import pallas as pl
from jax.experimental.pallas import tpu as pltpu
from jax.sharding import PartitionSpec as P

WIDTH = 128
MIB = 2**20
DIRECTS = (1, 1)
CROSSES = ()
PARTS = 3
GLUE_COST = 10**9
GAP = 2.1
ORDER = [(1, 0), (1, 1), ('L', 0), (1, 2), (2, 0), (1, 3), (2, 1), (1, 4), (2, 2), (3, 0), (2, 3), (3, 1), (2, 4), (3, 2), ('X', 0), (3, 3), ('X', 1), (3, 4), ('X', 2), ('X', 3), ('X', 4), ('L', 1), ('J', [(2, 0), (2, 1)]), ('L', 2), ('L', 3), ('J', [(0, 0), (0, 1), (0, 2)]), ('J', [(1, 0), (1, 1)]), ('J', [(1, 2)])]


NT = (((1,), (1,)), ((), ()))
TN = (((0,), (0,)), ((), ()))
VMEM = pl.BlockSpec(memory_space=pltpu.VMEM)
HBM = pl.BlockSpec(memory_space=pltpu.HBM)
ANY = pl.BlockSpec(memory_space=pl.ANY)
SMEM = pl.BlockSpec(memory_space=pltpu.SMEM)


def first_of(group, half, mine_ref):
    side = lax.rem(mine_ref[0], 2)
    return half * (side if group == 0 else 1 - side)


def rotated(seeds, first):
    heads = seeds.shape[0]
    return pltpu.roll(seeds, lax.rem(heads - first, heads), 0)


def table_of(row):
    square = jnp.broadcast_to(row, (WIDTH, WIDTH))
    return pltpu.roll(square, 0, 1, stride=1, stride_axis=0).astype(jnp.bfloat16)


def phi(x, table):
    mixed = jnp.dot(x, table, preferred_element_type=jnp.float32) * WIDTH ** (-0.25)
    return (jnp.exp(jnp.minimum(mixed, 0.0)) + jnp.maximum(mixed, 0.0)).astype(jnp.bfloat16)


def features(x, seeds, i):
    groups = seeds.shape[1] // WIDTH
    rows = [seeds[i : i + 1, g * WIDTH : (g + 1) * WIDTH] for g in range(groups)]
    return jnp.concatenate([phi(x, table_of(row)) for row in rows], axis=1)


def columns(head):
    if isinstance(head, int):
        return slice(head * WIDTH, (head + 1) * WIDTH)
    return pl.ds(pl.multiple_of(head * WIDTH, WIDTH), WIDTH)


def bounds(heads, parts):
    rows = heads * WIDTH
    cuts = [rows * n // parts // 8 * 8 for n in range(parts + 1)]
    return list(zip(cuts, cuts[1:]))


def overlaps(cuts, head):
    found = []
    for n, (low, high) in enumerate(cuts):
        start, stop = max(low, head * WIDTH), min(high, (head + 1) * WIDTH)
        if start < stop:
            found.append((n, slice(start - low, stop - low), slice(start, stop)))
    return found


def put_states(jobs):
    places = [(job, i) for job in jobs for i in range(job[1][-1][1] // WIDTH)]
    fks = [
        features(k_ref[:, columns(at + i)], seeds, base + at + i)
        for (_, _, seeds, base, at, k_ref, _), i in places
    ]
    states = [
        lax.dot_general(v_ref[:, columns(at + i)], fk, TN, preferred_element_type=jnp.float32)
        for ((_, _, _, _, at, _, v_ref), i), fk in zip(places, fks)
    ]
    sums = [jnp.sum(fk.astype(jnp.float32), axis=0, keepdims=True) for fk in fks]
    for ((outs, cuts, *_), i), state, total in zip(places, states, sums):
        size = cuts[0][1]
        if i == 0:
            outs[0][size:, :] = jnp.zeros(
                (outs[0].shape[0] - size, outs[0].shape[1]), jnp.float32
            )
        for n, rows, whole in overlaps(cuts, i):
            outs[n][rows, :] = state[whole.start - i * WIDTH : whole.stop - i * WIDTH, :]
        outs[0][size + i : size + i + 1, :] = total


def state_kernel(singles, cuts, which, places_ref, seeds_hbm, k_hbm, v_hbm, *refs):
    extra, refs = (refs[:1], refs[1:]) if which == 0 else ((), refs)
    half = cuts[-1][1] // WIDTH
    alone = sum(singles)
    outs, refs = refs[: len(singles) + len(cuts)], refs[len(singles) + len(cuts) :]
    gain_ref, refs = (refs[0], refs[1:]) if which == 0 else (None, refs)
    seeds_ref, k_ref, v_ref, kd_ref, vd_ref, sems = refs
    first = first_of(which, half, places_ref)
    span = pl.ds(pl.multiple_of(first * WIDTH, WIDTH), half * WIDTH)
    rest = pl.ds(2 * half * WIDTH, kd_ref.shape[1])
    pairs = [(seeds_hbm, seeds_ref)]
    if alone:
        pairs += [(k_hbm.at[:, rest], kd_ref), (v_hbm.at[:, rest], vd_ref)]
    pairs += [(gain_hbm, gain_ref) for gain_hbm in extra]
    pairs += [(k_hbm.at[:, span], k_ref), (v_hbm.at[:, span], v_ref)]
    copies = [pltpu.make_async_copy(a, b, sems.at[n]) for n, (a, b) in enumerate(pairs)]
    for copy in copies:
        copy.start()
    copies[0].wait()
    seeds = seeds_ref[...].astype(jnp.float32)
    for copy in copies[1:]:
        copy.wait()
    jobs, at = [], 0
    for n, size in enumerate(singles):
        jobs.append(([outs[n]], bounds(size, 1), seeds, 2 * half, at, kd_ref, vd_ref))
        at += size
    jobs.append((outs[len(singles) :], cuts, rotated(seeds, first), 0, 0, k_ref, v_ref))
    put_states(jobs)


def local_kernel(half, work, places_ref, _, seeds_ref, q_ref, k_ref, v_ref, *outs):
    tok = q_ref.shape[0]
    seeds = seeds_ref[...].astype(jnp.float32)
    rows = lax.broadcasted_iota(jnp.int32, (tok, tok), 0)
    causal = lax.broadcasted_iota(jnp.int32, (tok, tok), 1) <= rows
    places = []
    for group, i in work:
        if group == 2:
            places.append((2 * half + i, seeds, 2 * half + i))
        else:
            first = first_of(group, half, places_ref)
            places.append((first + i, rotated(seeds, first), i))
    fks = [features(k_ref[:, columns(head)], mine, i) for head, mine, i in places]
    fqs = [features(q_ref[:, columns(head)], mine, i) for head, mine, i in places]
    scores = [
        lax.dot_general(fq, fk, NT, preferred_element_type=jnp.float32)
        for fq, fk in zip(fqs, fks)
    ]
    scores = [jnp.where(causal, score, 0.0) for score in scores]
    nums = [
        jnp.dot(
            score.astype(jnp.bfloat16),
            v_ref[:, columns(head)],
            preferred_element_type=jnp.float32,
        )
        for score, (head, _, _) in zip(scores, places)
    ]
    dens = [jnp.sum(score, axis=1, keepdims=True) for score in scores]
    for n in range(len(work)):
        num_ref, den_ref, fq_ref = outs[3 * n : 3 * n + 3]
        fq_ref[...] = fqs[n]
        num_ref[...] = nums[n]
        den_ref[...] = jnp.broadcast_to(dens[n], (tok, WIDTH))


def send_kernel(places_ref, _, *refs):
    refs[-1][...] = functools.reduce(lambda a, b: a + b, [ref[...] for ref in refs[:-1]])


def pass_kernel(levels, crossed, places_ref, _, *refs):
    arrived, refs = refs[:levels], refs[levels:]
    own_ref = refs[-1]
    sent_ref, ours = (None, refs[:-1]) if crossed else (refs[-2], refs[:-2])
    prior = jnp.zeros(own_ref.shape, jnp.float32)
    for n, ref in enumerate(arrived):
        level = lax.div(places_ref[0], 2)
        prior = jnp.where(level == n + 1, ref[0 : prior.shape[0], :], prior)
    right = lax.rem(places_ref[0], 2) == 1
    if sent_ref is not None:
        sent_ref[...] = prior + jnp.where(right, 0.0, ours[0][...])
    own_ref[...] = prior + jnp.where(right, ours[1][...], 0.0) if len(ours) > 1 else prior


def join_kernel(half, work, final, places_ref, _, gain_ref, *refs):
    count = len(work)
    heads_refs, squares_ref = refs[-count - 1 : -1], refs[-1]
    wides, locals_ = [], []
    for _, _, cuts, n, copies in work:
        locals_.append(refs[:3])
        state, total = 0.0, 0.0
        refs = refs[3:]
        for _ in range(copies):
            parts, refs = refs[: len(cuts)], refs[len(cuts) :]
            rows = [parts[m][at, :] for m, at, _ in overlaps(cuts, n)]
            state = state + (rows[0] if len(rows) == 1 else jnp.concatenate(rows, axis=0))
            total = total + parts[0][cuts[0][1] + n : cuts[0][1] + n + 1, :]
        wides.append(jnp.concatenate([state, jnp.broadcast_to(total, state.shape)], axis=0))
    uppers = [wide.astype(jnp.bfloat16) for wide in wides]
    lowers = [
        (wide - upper.astype(jnp.float32)).astype(jnp.bfloat16)
        for wide, upper in zip(wides, uppers)
    ]
    fqs = [local[2][...] for local in locals_]
    boths = [
        lax.dot_general(fq, upper, NT, preferred_element_type=jnp.float32)
        + lax.dot_general(fq, lower, NT, preferred_element_type=jnp.float32)
        for fq, upper, lower in zip(fqs, uppers, lowers)
    ]
    heads = [
        (num_ref[...] + both[:, :WIDTH]) / (den_ref[...] + both[:, WIDTH:])
        for (num_ref, den_ref, _), both in zip(locals_, boths)
    ]
    squares = functools.reduce(lambda a, b: a + b, [head * head for head in heads])
    for (group, i, *_), out_ref, head in zip(work, heads_refs, heads):
        place = 2 * half + i if group == 2 else first_of(group, half, places_ref) + i
        out_ref[...] = head * gain_ref[:, columns(place)]
    if len(refs) > count + 1:
        squares = squares + refs[0][...]
    if final:
        squares = jnp.broadcast_to(jnp.sum(squares, axis=1, keepdims=True), squares.shape).T[0:8, :]
    squares_ref[...] = squares


def norm_kernel(half, entries, work, places_ref, *refs):
    heads, squares, out_ref = refs[: len(work)], refs[len(work) : -1], refs[-1]
    tok = out_ref.shape[0]
    overall = functools.reduce(lambda a, b: a + b, [ref[...] for ref in squares])
    factor = lax.rsqrt(overall / entries + 1e-06)
    wide = jnp.broadcast_to(factor[0:1, :], (WIDTH, tok)).T
    for (group, i), source in zip(work, heads):
        place = 2 * half + i if group == 2 else first_of(group, half, places_ref) + i
        out_ref[:, columns(place)] = (source[...] * wide).astype(jnp.bfloat16)


def call(kernel, outs, ins, flops, scratch=(), specs=(), place=VMEM, limit=16 * MIB):
    moved = sum(x.size * x.dtype.itemsize for x in ins)
    moved += sum(x.size * jnp.dtype(x.dtype).itemsize for x in jax.tree.leaves(outs))
    return pl.pallas_call(
        kernel,
        out_shape=outs,
        in_specs=[SMEM, *specs] + [place] * (len(ins) - 1 - len(specs)),
        out_specs=jax.tree.map(lambda _: VMEM, outs),
        scratch_shapes=list(scratch),
        compiler_params=pltpu.CompilerParams(vmem_limit_bytes=limit),
        cost_estimate=pl.CostEstimate(flops=flops, bytes_accessed=moved, transcendentals=0),
    )(*ins)


def per_device(queries, keys, values, seeds, gain):
    f32, bf16 = jnp.float32, jnp.bfloat16
    tok = queries.shape[0]
    heads, feats = seeds.shape
    singles = DIRECTS + CROSSES
    alone = sum(singles)
    half = (heads - alone) // 2
    count = lax.axis_size("seq")
    depth = count // 2
    across = lax.axis_size("tp")
    mine = lax.axis_index("seq")
    places = mine.reshape(1)
    shape = lambda *dims, dtype=f32: jax.ShapeDtypeStruct(dims, dtype)
    cuts = bounds(half, PARTS)

    def state_shapes(cuts):
        return [shape(b - a + (8 if a == 0 else 0), feats) for a, b in cuts]

    def states(singles, which, limit):
        part = pltpu.VMEM((tok, half * WIDTH), keys.dtype)
        rest = pltpu.VMEM((tok, max(1, alone) * WIDTH), keys.dtype)
        return call(
            functools.partial(state_kernel, singles, cuts, which),
            [x for size in singles for x in state_shapes(bounds(size, 1))]
            + state_shapes(cuts)
            + ([shape(1, heads * WIDTH)] if which == 0 else []),
            (places, seeds, keys, values, *([gain.reshape(1, -1)] if which == 0 else [])),
            (sum(singles) + half) * tok * feats * WIDTH * 4,
            [pltpu.VMEM(seeds.shape, seeds.dtype), part, part, rest, rest]
            + [pltpu.SemaphoreType.DMA((5,))],
            place=HBM,
            limit=limit,
        )

    swap = [(i, i ^ 1) for i in range(count)]
    first = states(singles, 1, 60 * MIB)
    direct, cross = first[: len(DIRECTS)], first[len(DIRECTS) : len(singles)]
    theirs = first[len(singles) :]
    incoming = [lax.ppermute(part, "seq", swap) for part in [*theirs, *cross]]
    *ours, gain = states((), 0, 40 * MIB)
    chunks = [*[(part,) for part in direct], *zip([*ours, *cross], incoming)]
    total = len(chunks)
    locals_, arrivals, own, passed = {}, {}, [None] * total, [None] * total
    work = [[(2, i) for i in range(alone)][n : n + 2] for n in range(0, alone, 2)]
    work += [[(0, i), (1, i)] for i in range(half)]
    homes = [(n, i) for n, size in enumerate(singles) for i in range(size)]
    last = places

    def hop(stage, i):
        nonlocal last
        parts = chunks[i] if stage == 1 else (arrivals[stage - 1, i], *chunks[i])
        sent = parts[0]
        if len(parts) > 1:
            sent = call(
                send_kernel,
                shape(*sent.shape),
                (places, last, *parts),
                GLUE_COST,
                specs=[ANY],
            )
            last = sent
        pairs = [(2 * stage - 2 + s, 2 * stage + s) for s in range(2)]
        arrivals[stage, i] = lax.ppermute(sent, "seq", pairs)

    def hand(i):
        nonlocal last
        crossed = i >= len(DIRECTS) + PARTS
        like = shape(*chunks[i][0].shape)
        came = [arrivals[z, i] for z in range(1, depth)]
        *sent, own[i] = call(
            functools.partial(pass_kernel, depth - 1, crossed),
            [like] if crossed else [like, like],
            (places, last, *came, *chunks[i]),
            GLUE_COST,
            specs=[ANY],
        )
        last = own[i] if crossed else sent[0]
        if not crossed:
            passed[i] = lax.ppermute(last, "seq", swap)

    def local(piece):
        nonlocal last
        shapes = [shape(tok, WIDTH), shape(tok, WIDTH), shape(tok, feats, dtype=bf16)]
        parts = call(
            functools.partial(local_kernel, half, work[piece]),
            shapes * len(work[piece]),
            (places, last, seeds, queries, keys, values),
            len(work[piece]) * tok * (feats * WIDTH * 4 + tok * (feats + WIDTH) * 2),
            specs=[ANY],
        )
        last = parts[0]
        for n, key in enumerate(work[piece]):
            locals_[key] = parts[3 * n : 3 * n + 3]

    results, squares = {}, None

    def join(todo):
        nonlocal last, squares
        final = len(results) + len(todo) == heads
        plan, ins = [], []
        for group, i in todo:
            if group == 2:
                n, at = homes[i]
                plan.append((2, i, bounds(singles[n], 1), at, 2 if n < len(DIRECTS) else 1))
                if n < len(DIRECTS):
                    arrays = [own[n], passed[n]]
                else:
                    arrays = [own[n + PARTS]]
            else:
                arrays = (own if group == 0 else passed)[len(DIRECTS) : len(DIRECTS) + PARTS]
                used = max(n for n, _, _ in overlaps(cuts, i)) + 1
                plan.append((group, i, cuts[:used], i, 1))
                arrays = arrays[:used]
            ins += [*locals_[group, i], *arrays]
        *outs, squares = call(
            functools.partial(join_kernel, half, plan, final),
            [shape(tok, WIDTH)] * len(todo) + [shape(8, tok) if final else shape(tok, WIDTH)],
            (places, last, gain, *ins, *([] if squares is None else [squares])),
            len(todo) * tok * feats * WIDTH * 8,
            specs=[ANY],
        )
        last = squares
        results.update(zip(todo, outs))

    hops = [
        (i + GAP * (stage - 1), stage, i) for stage in range(1, depth + 1) for i in range(total)
    ]
    order = [("X" if stage == depth else stage, i) for _, stage, i in sorted(hops)]
    if ORDER and depth == 4 and total == 5:
        order = ORDER
    singles_done = [(2, i) for i in range(alone)]
    rest = [("L", i) for i in range(len(work))]
    rest += [("J", singles_done), ("J", [(0, i) for i in range(half)])]
    rest += [("J", [(1, i) for i in range(half - 1)]), ("J", [(1, half - 1)])]
    for kind, i in [*order, *rest]:
        if kind == "X":
            hand(i)
        elif kind == "L":
            if work[i][0] not in locals_:
                local(i)
        elif kind == "J":
            if i and i[0] not in results:
                join(i)
        else:
            hop(kind, i)
    gathered = [squares] + [
        lax.ppermute(squares, "tp", [(i, (i ^ k) if across == 4 else (i + k) % across) for i in range(across)])
        for k in range(across - 1, 0, -1)
    ]
    return call(
        functools.partial(norm_kernel, half, heads * WIDTH * across, list(results)),
        shape(tok, heads * WIDTH, dtype=bf16),
        (places, *results.values(), *gathered),
        tok * heads * WIDTH * 3,
    )


def solution(mesh):
    placed = (P("seq", "tp"), P("seq", "tp"), P("seq", "tp"), P("tp", None), P("tp"))
    return jax.shard_map(
        per_device, mesh=mesh, in_specs=placed, out_specs=P("seq", "tp"), check_vma=False
    )
```
